256 devices in a mesh: section: 16 (over y, z_lo), dp: 16 (over x, z_hi, core).
Axes of the slice: x: 4, y: 4, z: 8 (z_hi: 2, z_lo: 4; z = z_hi * 4 + z_lo), core: 2. Of those that a mesh axis runs over, the one named last changes fastest.
Arguments:
- latents: bfloat16 [2, 16, 8, 8, 640], P(None, 'dp'), may hold values from -6 to 6
- cotangent: bfloat16 [2, 16, 8, 8, 640], P(None, 'dp'), may hold values from -6 to 6
- conv_weight: bfloat16 [16, 3, 3, 640, 640], P('section'), may hold values from -0.078125 to 0.078125
- timesteps: int32 [2, 16], P(None, 'dp'), may hold values from 0 to 999
- time_table: float32 [1000, 640], replicated, may hold values from -6 to 6
Outputs:
- weight_grads: float32 [16, 3, 3, 640, 640], P('section', None, None, None, 'dp')
The draws below stay inside these ranges and needn't reach their ends.
All inputs are finite; a program needn't handle non-finite values.
Results may differ from the reference program's by a relative error of at most 0.027.
Values may be sent and summed in bfloat16 or wider, within the bound.
A program may use at most 128 MiB of HBM per device.

```python
import math
import jax
import jax.numpy as jnp
from jax import lax

C = 640
TSTEPS = 1000
SIDE = 8
MICRO = 2
SAMPLES_DEV = 1
SAMPLES = 16
LEVELS = 16


def place_ends(entries, own_key, low, top_value):
    longest = entries.shape.index(max(entries.shape))
    spots = []
    for shift in (0, 1):
        where = [jax.random.randint(jax.random.fold_in(own_key, axis), (), 0, length) for axis, length in enumerate(entries.shape)]
        where[longest] = (where[longest] + shift) % entries.shape[longest]
        spots.append(tuple(where))
    return entries.at[spots[0]].set(low).at[spots[1]].set(top_value)


def block_scale(stream_key, shape, split, least, high):
    factor_of, own = 1.0, jax.random.fold_in(stream_key, 6)
    for position, parts in split:
        steps = jnp.exp(jax.random.uniform(jax.random.fold_in(own, position), (parts,), jnp.float32, least / len(split), high / len(split)))
        factor_of = factor_of * jnp.repeat(steps, shape[position] // parts).reshape([-1 if axis == position else 1 for axis in range(len(shape))])
    return factor_of


def gaussian(stream_key, dims, spread, limit, cuts=(), dtype=jnp.bfloat16):
    values = spread * jax.random.normal(stream_key, dims, jnp.float32)
    if cuts:
        values = values * block_scale(stream_key, dims, cuts, -0.22, 0.18)
    return jnp.clip(values, -limit, limit).astype(dtype)


def setup_inputs(seed: int = 0) -> dict:
    arg_keys = jax.random.split(jax.random.key(seed), 6)
    return {
        "latents": gaussian(arg_keys[0], (MICRO, SAMPLES, SIDE, SIDE, C), 1.0, 6.0, ((1, 16),)),
        "cotangent": gaussian(arg_keys[1], (MICRO, SAMPLES, SIDE, SIDE, C), 1.0, 6.0, ((1, 16),)),
        "conv_weight": gaussian(arg_keys[2], (LEVELS, 3, 3, C, C), (9 * C) ** -0.5, 0.078125, ((0, 16),)),
        "timesteps": place_ends(jax.random.randint(arg_keys[3], (MICRO, SAMPLES), 0, TSTEPS), jax.random.fold_in(arg_keys[3], 1), 0, TSTEPS - 1).astype(jnp.int32),
        "time_table": gaussian(arg_keys[4], (TSTEPS, C), 1.0, 6.0, (), jnp.float32),
    }


EPS = 1e-05

def normalize(inputs):
    inv_rms = lax.rsqrt(lax.optimization_barrier(jnp.mean(inputs * inputs, axis=-1, keepdims=True)) + EPS)
    return (inv_rms, inputs * inv_rms)

def conv_forward(normed_b, weight):
    return lax.conv_general_dilated(normed_b.astype(jnp.float32), weight.astype(jnp.float32), (1, 1), 'SAME', dimension_numbers=('NHWC', 'HWIO', 'NHWC'), precision=lax.Precision.HIGHEST)

def conv_input_grad(grad_b, weight):
    flipped = weight[::-1, ::-1].astype(jnp.float32)
    return lax.conv_general_dilated(grad_b.astype(jnp.float32), flipped, (1, 1), 'SAME', dimension_numbers=('NHWC', 'HWOI', 'NHWC'), precision=lax.Precision.HIGHEST)

def grouped_weight_grad(normed_b, grad_b, micro_count, group_count):
    total, side_h, side_w, chans = normed_b.shape
    padded = jnp.pad(normed_b.astype(jnp.float32), ((0, 0), (1, 1), (1, 1), (0, 0)))
    grad_f = grad_b.astype(jnp.float32).reshape(micro_count, group_count, SAMPLES_DEV, side_h, side_w, chans)
    kernel_rows = []
    for shift_h in range(3):
        kernel_cols = []
        for shift_w in range(3):
            window = padded[:, shift_h:shift_h + side_h, shift_w:shift_w + side_w, :]
            window = window.reshape(micro_count, group_count, SAMPLES_DEV, side_h, side_w, chans)
            partial_value = jnp.einsum('mgshwi,mgshwo->gio', window, grad_f, precision=lax.Precision.HIGHEST)
            rounded = lax.optimization_barrier(partial_value.astype(jnp.bfloat16)).astype(jnp.float32)
            kernel_cols.append(lax.optimization_barrier(jnp.sum(rounded, axis=0)))
        kernel_rows.append(jnp.stack(kernel_cols))
    return jnp.stack(kernel_rows)

def level_forward(inputs, weight, t_embed):
    inv_rms, normed = normalize(inputs)
    pre_act = conv_forward(normed.astype(jnp.bfloat16), weight) + t_embed[:, None, None, :]
    branch = pre_act * jax.nn.sigmoid(pre_act)
    return ((inputs + branch).astype(jnp.bfloat16), branch.astype(jnp.bfloat16), pre_act)

def level_backward(inputs, weight, pre_act, grad_out, grad_branch, micro_count, group_count):
    inv_rms, normed = normalize(inputs)
    normed_b = normed.astype(jnp.bfloat16)
    sigmoid_pre = jax.nn.sigmoid(pre_act)
    grad_pre = (grad_branch * sigmoid_pre * (1.0 + pre_act * (1.0 - sigmoid_pre))).astype(jnp.bfloat16)
    weight_grad = grouped_weight_grad(normed_b, grad_pre, micro_count, group_count)
    grad_normed = conv_input_grad(grad_pre, weight)
    grad_in = grad_out + inv_rms * (grad_normed - normed * lax.optimization_barrier(jnp.mean(grad_normed * normed, axis=-1, keepdims=True)))
    return (grad_in.astype(jnp.bfloat16), weight_grad)

def reference(latents, cotangent, conv_weight, timesteps, time_table):
    level_count = conv_weight.shape[0]
    half_count = level_count // 2
    micro_count, sample_count, side_h, side_w, chans = latents.shape
    group_count = sample_count // SAMPLES_DEV
    batch_count = micro_count * sample_count
    t_embed = time_table[timesteps.reshape(batch_count).astype(jnp.int32)]
    hidden = latents.reshape(batch_count, side_h, side_w, chans)
    saved_inputs = []
    saved_pre = []
    skips = []
    for level_index in range(level_count):
        inputs = hidden.astype(jnp.float32)
        if level_index >= half_count:
            inputs = inputs + skips[level_count - 1 - level_index].astype(jnp.float32)
        hidden, branch, pre_act = level_forward(inputs, conv_weight[level_index], t_embed)
        if level_index < half_count:
            skips.append(branch)
        saved_inputs.append(inputs)
        saved_pre.append(pre_act)
    grad_hidden = cotangent.reshape(batch_count, side_h, side_w, chans)
    skip_grads = [None] * half_count
    weight_grads = [None] * level_count
    for level_index in reversed(range(level_count)):
        grad_out = grad_hidden.astype(jnp.float32)
        if level_index >= half_count:
            grad_branch = grad_out
        else:
            grad_branch = grad_out + skip_grads[level_index].astype(jnp.float32)
        grad_hidden, weight_grad = level_backward(saved_inputs[level_index], conv_weight[level_index], saved_pre[level_index], grad_out, grad_branch, micro_count, group_count)
        if level_index >= half_count:
            skip_grads[level_count - 1 - level_index] = grad_hidden
        weight_grads[level_index] = weight_grad
    row_total = micro_count * sample_count * side_h * side_w
    return jnp.stack(weight_grads) / math.sqrt(row_total)
```

```python
import math

import jax
import jax.numpy as jnp
from jax import lax
from jax.experimental import pallas as pl
from jax.experimental.pallas import tpu as pltpu
from jax.sharding import PartitionSpec as P

EPS = 1e-05
SIDE = 8
PIX = SIDE * SIDE
ROWS = 48


def gather_taps(value, store):
    chans = value.shape[1]
    col = lax.broadcasted_iota(jnp.int32, (PIX, 1), 0) % SIDE
    edge = jnp.zeros((SIDE, chans), jnp.float32)
    left = jnp.where(col > 0, pltpu.roll(value, 1, 0), 0.0)
    right = jnp.where(col < SIDE - 1, pltpu.roll(value, PIX - 1, 0), 0.0)
    for kw, v in enumerate((left, value, right)):
        store(kw, jnp.concatenate([edge, v[: PIX - SIDE]], 0).astype(jnp.bfloat16))
        store(3 + kw, v.astype(jnp.bfloat16))
        store(6 + kw, jnp.concatenate([v[SIDE:], edge], 0).astype(jnp.bfloat16))


def column_blocks(chans):
    return [(a, min(a + 256, chans)) for a in range(0, chans, 256)]


def make_kernel(sections, replicas, chans, share, scale):
    half = sections // 2
    xs = replicas // 4

    def kernel(
        times_ref, lat_ref, cot_ref, w_hbm, table_hbm, out_ref,
        w, wt, table, lhs, inbox, skip, fout, sout, gin, dskip, gout,
        normed, inv, slope, gpre, gtrans, pack, shares, gathered, amat,
        load_sem, in_sem, f_send, f_recv, s_send, s_recv, g_send, g_recv, d_send, d_recv,
        a_send, a_recv, b_send, b_recv, c_send, c_recv, p_send, p_recv,
    ):
        s = lax.axis_index("section")
        d = lax.axis_index("dp")
        core = lax.rem(d, 2)
        zh = lax.rem(d // 2, 2)
        x = d // 4
        place = core * (replicas // 2) + x * 2 + zh

        def at(dst_s, dst_d):
            return {"section": dst_s, "dp": dst_d}

        def replica(px, pz, pc):
            return px * 4 + pz * 2 + pc

        nxt = jnp.minimum(s + 1, sections - 1)
        prv = jnp.maximum(s - 1, 0)
        mir = sections - 1 - s
        first, last = s == 0, s == sections - 1
        far = (s != half - 1) & (s != half)

        load_w = pltpu.make_async_copy(w_hbm, w, load_sem.at[0])
        load_t = pltpu.make_async_copy(table_hbm, table, load_sem.at[1])
        load_w.start()
        load_t.start()

        barrier = pltpu.get_barrier_semaphore()

        def greet(k, _):
            to = lax.rem(d + k, replicas)
            pl.semaphore_signal(barrier, inc=1, device_id=at(s, to))
            return None

        lax.fori_loop(1, replicas, greet, None)

        @pl.when(jnp.logical_not(first))
        def _():
            pl.semaphore_signal(barrier, inc=1, device_id=at(prv, d))

        @pl.when(jnp.logical_not(last))
        def _():
            pl.semaphore_signal(barrier, inc=1, device_id=at(nxt, d))

        @pl.when(far)
        def _():
            pl.semaphore_signal(barrier, inc=1, device_id=at(mir, d))

        @pl.when(first)
        def _():
            load = pltpu.make_async_copy(lat_ref, inbox, in_sem)
            load.start()
            load.wait()

        @pl.when(last)
        def _():
            load = pltpu.make_async_copy(cot_ref, gin, in_sem)
            load.start()
            load.wait()

        @pl.when(s <= half)
        def _():
            skip[...] = jnp.zeros_like(skip)

        @pl.when(s >= half - 1)
        def _():
            dskip[...] = jnp.zeros_like(dskip)

        load_w.wait()
        load_t.wait()
        pl.semaphore_wait(
            barrier,
            replicas - 1
            + jnp.where(first, 0, 1)
            + jnp.where(last, 0, 1)
            + jnp.where(far, 1, 0),
        )

        def turn_weights():
            def turn(t, _):
                src = pl.multiple_of(t * chans, chans)
                dst = pl.multiple_of((8 - t) * chans, chans)
                for r in range(0, chans, 128):
                    block = w[pl.ds(src + r, 128), :]
                    wt[pl.ds(dst, chans), r : r + 128] = block.T
                return None

            lax.fori_loop(0, 9, turn, None)

        early = s >= 4

        @pl.when(early)
        def _():
            turn_weights()

        def put(t, v):
            lhs[:, t * chans : (t + 1) * chans] = v

        def copy_f(m):
            return pltpu.make_async_remote_copy(
                src_ref=fout.at[m], dst_ref=inbox.at[m], send_sem=f_send.at[m], recv_sem=f_recv.at[m],
                device_id=at(nxt, d))

        def copy_s(m):
            return pltpu.make_async_remote_copy(
                src_ref=sout.at[m], dst_ref=skip.at[m], send_sem=s_send.at[m], recv_sem=s_recv.at[m],
                device_id=at(mir, d))

        def copy_g(m):
            return pltpu.make_async_remote_copy(
                src_ref=gout.at[m], dst_ref=gin.at[m], send_sem=g_send.at[m], recv_sem=g_recv.at[m],
                device_id=at(prv, d))

        def copy_d(m):
            return pltpu.make_async_remote_copy(
                src_ref=gout.at[m], dst_ref=dskip.at[m], send_sem=d_send.at[m], recv_sem=d_recv.at[m],
                device_id=at(mir, d))

        def forward(m, _):
            @pl.when(jnp.logical_not(first))
            def _():
                copy_f(m).wait_recv()

            @pl.when(s > half)
            def _():
                copy_s(m).wait_recv()

            value = inbox[m].astype(jnp.float32) + skip[m].astype(jnp.float32)
            inv_rms = lax.rsqrt(jnp.mean(value * value, axis=-1, keepdims=True) + EPS)
            norm = value * inv_rms
            gather_taps(norm, put)
            step = times_ref[m, 0]
            emb = table[pl.ds(step, 1), :]
            for a, b in column_blocks(chans):
                pre = jnp.dot(lhs[...], w[:, a:b], preferred_element_type=jnp.float32) + emb[:, a:b]
                sig = jax.nn.sigmoid(pre)
                branch = pre * sig
                result = value[:, a:b] + branch
                branch_b = branch.astype(jnp.bfloat16)
                result = result.astype(jnp.bfloat16).astype(jnp.float32)
                result = result + jnp.where(s == half - 1, branch_b.astype(jnp.float32), 0.0)
                fout[m, :, a:b] = result.astype(jnp.bfloat16)
                sout[m, :, a:b] = branch_b
                slope[m, :, a:b] = sig * (1.0 + pre * (1.0 - sig))

            @pl.when(jnp.logical_not(last))
            def _():
                copy_f(m).start()

            @pl.when(s < half - 1)
            def _():
                copy_s(m).start()

            normed[m] = norm
            inv[m] = jnp.broadcast_to(inv_rms, (PIX, 128))
            gathered[place, pl.ds(pl.multiple_of(m * PIX, PIX), PIX), :] = norm.astype(jnp.bfloat16)
            return None

        lax.fori_loop(0, 2, forward, None)

        @pl.when(jnp.logical_not(early))
        def _():
            turn_weights()

        def copy_a():
            mine = gathered.at[place]
            return pltpu.make_async_remote_copy(
                src_ref=mine, dst_ref=mine, send_sem=a_send, recv_sem=a_recv,
                device_id=at(s, replica(x, 1 - zh, core)))

        def copy_b(k):
            mine = gathered.at[pl.ds(core * (replicas // 2) + x * 2, 2)]
            return pltpu.make_async_remote_copy(
                src_ref=mine, dst_ref=mine, send_sem=b_send.at[k - 1], recv_sem=b_recv.at[k - 1],
                device_id=at(s, replica(lax.rem(x + k, xs), zh, core)))

        def wait_b(k):
            theirs = lax.rem(x + xs - k, xs)
            part = gathered.at[pl.ds(core * (replicas // 2) + theirs * 2, 2)]
            pltpu.make_async_remote_copy(
                src_ref=part, dst_ref=part, send_sem=b_send.at[k - 1], recv_sem=b_recv.at[k - 1],
                device_id=at(s, replica(theirs, zh, core))).wait_recv()

        def copy_c(c):
            part = gathered.at[pl.ds(c * (replicas // 2), replicas // 2)]
            return pltpu.make_async_remote_copy(
                src_ref=part, dst_ref=part, send_sem=c_send, recv_sem=c_recv,
                device_id=at(s, replica(x, zh, 1 - core)))

        def gather_all():
            theirs = gathered.at[core * (replicas // 2) + x * 2 + (1 - zh)]
            copy_a().start()
            pltpu.make_async_remote_copy(
                src_ref=theirs, dst_ref=theirs, send_sem=a_send, recv_sem=a_recv,
                device_id=at(s, replica(x, 1 - zh, core))).wait_recv()
            for k in range(1, xs):
                copy_b(k).start()
            for k in range(1, xs):
                wait_b(k)
            copy_c(core).start()
            copy_c(1 - core).wait_recv()
            copy_a().wait_send()
            for k in range(1, xs):
                copy_b(k).wait_send()
            copy_c(core).wait_send()

        soon = s < sections - 3

        @pl.when(soon)
        def _():
            gather_all()

        factor = jnp.where(s == half - 1, 2.0, 1.0).astype(jnp.float32)

        def backward(m, _):
            @pl.when(jnp.logical_not(last))
            def _():
                copy_g(m).wait_recv()

            @pl.when(s < half - 1)
            def _():
                copy_d(m).wait_recv()

            grad = gin[m].astype(jnp.float32)
            branch_grad = grad * factor + dskip[m].astype(jnp.float32)
            grad_pre = (branch_grad * slope[m]).astype(jnp.bfloat16).astype(jnp.float32)
            gather_taps(grad_pre, put)
            gpre[pl.ds(pl.multiple_of(m * PIX, PIX), PIX), :] = grad_pre
            parts = [
                jnp.dot(lhs[...], wt[:, a:b], preferred_element_type=jnp.float32)
                for a, b in column_blocks(chans)
            ]
            gn = jnp.concatenate(parts, axis=1)
            norm = normed[m]
            inner = jnp.mean(gn * norm, axis=-1, keepdims=True)
            gout[m] = (grad + inv[m][:, :1] * (gn - norm * inner)).astype(jnp.bfloat16)

            @pl.when(jnp.logical_not(first))
            def _():
                copy_g(m).start()

            @pl.when(s > half)
            def _():
                copy_d(m).start()

            return None

        lax.fori_loop(0, 2, backward, None)

        for r in range(0, chans, 128):
            gtrans[r : r + 128, :] = gpre[:, r : r + 128].T
        pad = jnp.zeros((ROWS - share, 2 * PIX), jnp.float32)
        for j in range(replicas):
            part = jnp.concatenate([gtrans[share * j : share * (j + 1), :], pad], 0)
            pack[j] = part.astype(jnp.bfloat16)

        def copy_p(to):
            return pltpu.make_async_remote_copy(
                src_ref=pack.at[to], dst_ref=shares.at[place], send_sem=p_send.at[to],
                recv_sem=p_recv.at[place], device_id=at(s, to))

        def send_share(k, _):
            copy_p(lax.rem(d + k, replicas)).start()
            return None

        lax.fori_loop(1, replicas, send_share, None)
        shares[place] = pack[d]

        @pl.when(jnp.logical_not(soon))
        def _():
            gather_all()

        def wait_share(k, _):
            slot = lax.rem(place + k, replicas)
            pltpu.make_async_remote_copy(
                src_ref=pack.at[0], dst_ref=shares.at[slot], send_sem=p_send.at[0],
                recv_sem=p_recv.at[slot], device_id=at(s, lax.rem(d + 1, replicas))).wait_recv()
            return None

        lax.fori_loop(1, replicas, wait_share, None)

        lane = lax.broadcasted_iota(jnp.int32, (1, 2 * PIX), 1)
        row, col = (lane // SIDE) % SIDE, lane % SIDE
        keep = []
        for kh in range(3):
            for kw in range(3):
                r, c = row - (kh - 1), col - (kw - 1)
                keep.append((r >= 0) & (r < SIDE) & (c >= 0) & (c < SIDE))
        for b in range(replicas):
            block = shares[b].astype(jnp.float32)
            for t in range(9):
                shift = (SIDE * (t // 3 - 1) + t % 3 - 1) % (2 * PIX)
                moved = pltpu.roll(block, shift, 1) if shift else block
                moved = jnp.where(keep[t], moved, 0.0)
                amat[ROWS * t : ROWS * (t + 1), 2 * PIX * b : 2 * PIX * (b + 1)] = moved.astype(jnp.bfloat16)
        rhs = gathered[...].reshape(replicas * 2 * PIX, chans)
        for a, b in column_blocks(chans):
            total = jnp.dot(amat[...], rhs[:, a:b], preferred_element_type=jnp.float32) * scale
            for t in range(9):
                out_ref[t, :, a:b] = total[ROWS * t : ROWS * t + share]

        def drain(m, _):
            @pl.when(jnp.logical_not(last))
            def _():
                copy_f(m).wait_send()

            @pl.when(s < half - 1)
            def _():
                copy_s(m).wait_send()

            @pl.when(jnp.logical_not(first))
            def _():
                copy_g(m).wait_send()

            @pl.when(s > half)
            def _():
                copy_d(m).wait_send()

            return None

        lax.fori_loop(0, 2, drain, None)

        def drain_share(k, _):
            copy_p(lax.rem(d + k, replicas)).wait_send()
            return None

        lax.fori_loop(1, replicas, drain_share, None)

    return kernel


def on_device(latents, cotangent, conv_weight, timesteps, time_table):
    sections = lax.axis_size("section")
    replicas = lax.axis_size("dp")
    micro, samples, side_h, side_w, chans = latents.shape
    share = chans // replicas
    scale = 1.0 / math.sqrt(micro * samples * replicas * side_h * side_w)
    fields = (micro, PIX, chans)
    dma = pltpu.SemaphoreType.DMA
    anyspace = pl.BlockSpec(memory_space=pl.ANY)
    bf, f32 = jnp.bfloat16, jnp.float32
    out = pl.pallas_call(
        make_kernel(sections, replicas, chans, share, scale),
        out_shape=jax.ShapeDtypeStruct((9, share, chans), f32),
        in_specs=[pl.BlockSpec(memory_space=pltpu.SMEM), anyspace, anyspace, anyspace, anyspace],
        out_specs=pl.BlockSpec(memory_space=pltpu.VMEM),
        scratch_shapes=[
            pltpu.VMEM((9 * chans, chans), bf),
            pltpu.VMEM((9 * chans, chans), bf),
            pltpu.VMEM(time_table.shape, f32),
            pltpu.VMEM((PIX, 9 * chans), bf),
            pltpu.VMEM(fields, bf),
            pltpu.VMEM(fields, bf),
            pltpu.VMEM(fields, bf),
            pltpu.VMEM(fields, bf),
            pltpu.VMEM(fields, bf),
            pltpu.VMEM(fields, bf),
            pltpu.VMEM(fields, bf),
            pltpu.VMEM(fields, f32),
            pltpu.VMEM((micro, PIX, 128), f32),
            pltpu.VMEM(fields, f32),
            pltpu.VMEM((micro * PIX, chans), f32),
            pltpu.VMEM((chans, micro * PIX), f32),
            pltpu.VMEM((replicas, ROWS, micro * PIX), bf),
            pltpu.VMEM((replicas, ROWS, micro * PIX), bf),
            pltpu.VMEM((replicas, micro * PIX, chans), bf),
            pltpu.VMEM((9 * ROWS, replicas * micro * PIX), bf),
            dma((2,)), dma, dma((2,)), dma((2,)), dma((2,)), dma((2,)), dma((2,)), dma((2,)), dma((2,)), dma((2,)),
            dma, dma, dma((replicas // 4 - 1,)), dma((replicas // 4 - 1,)), dma, dma,
            dma((replicas,)), dma((replicas,)),
        ],
        compiler_params=pltpu.CompilerParams(
            collective_id=0, has_side_effects=True, vmem_limit_bytes=56 * 2**20
        ),
        name="levels",
    )(
        timesteps,
        latents.reshape(fields),
        cotangent.reshape(fields),
        conv_weight.reshape(9 * chans, chans),
        time_table,
    )
    return jnp.swapaxes(out, 1, 2).reshape(1, 3, 3, chans, share)


def solution(mesh):
    in_specs = (
        P(None, "dp", None, None, None),
        P(None, "dp", None, None, None),
        P("section", None, None, None, None),
        P(None, "dp"),
        P(),
    )
    out_specs = P("section", None, None, None, "dp")
    return jax.shard_map(
        on_device, mesh=mesh, in_specs=in_specs, out_specs=out_specs, check_vma=False
    )
```

```python
import math

import jax
import jax.numpy as jnp
from jax import lax
from jax.experimental import pallas as pl
from jax.experimental.pallas import tpu as pltpu
from jax.sharding import PartitionSpec as P

EPS = 1e-05
SIDE = 8
PIX = SIDE * SIDE
PAIR_FROM = 8
PACK_ROWS = 32
ROWS = 48


def gather_taps(value, store):
    chans = value.shape[1]
    col = lax.broadcasted_iota(jnp.int32, (PIX, 1), 0) % SIDE
    edge = jnp.zeros((SIDE, chans), jnp.float32)
    left = jnp.where(col > 0, pltpu.roll(value, 1, 0), 0.0)
    right = jnp.where(col < SIDE - 1, pltpu.roll(value, PIX - 1, 0), 0.0)
    for kw, v in enumerate((left, value, right)):
        store(kw, jnp.concatenate([edge, v[: PIX - SIDE]], 0).astype(jnp.bfloat16))
        store(3 + kw, v.astype(jnp.bfloat16))
        store(6 + kw, jnp.concatenate([v[SIDE:], edge], 0).astype(jnp.bfloat16))


def column_blocks(chans):
    return [(a, min(a + 256, chans)) for a in range(0, chans, 256)]


def make_kernel(sections, replicas, chans, share, scale, pair_from):
    half = sections // 2
    xs = replicas // 4
    lanes = 2 * PIX
    taps = 9 * chans

    def kernel(
        times_hbm, lat_ref, cot_ref, w_hbm, table_hbm, out_ref,
        times, w, wt, table, lhs, inbox, skip, fout, sout, gin, dskip, gout,
        state, gpre, gtrans, pack, shares, gathered, nstage, amat,
        load_sem, in_sem, f_send, f_recv, s_send, s_recv, g_send, g_recv, d_send, d_recv,
        a_send, a_recv, b_send, b_recv, c_send, c_recv, p_send, p_recv,
        n_send, n_recv, t_send, t_recv, z_send, z_recv, x_send, x_recv, y_send, y_recv, go,
    ):
        s = lax.axis_index("section")
        d = lax.axis_index("dp")
        core = lax.rem(d, 2)
        zh = lax.rem(d // 2, 2)
        x = d // 4
        place = core * (replicas // 2) + x * 2 + zh
        pair, e = s // 2, lax.rem(s, 2)
        mate = s + 1 - 2 * e
        line_len = 4
        line = lax.rem(s, line_len)
        top_line = s >= sections - line_len
        hop = s < pair_from

        def at(dst_s, dst_d):
            return {"section": dst_s, "dp": dst_d}

        def replica(px, pz, pc):
            return px * 4 + pz * 2 + pc

        def remote(src, dst, send, recv, dst_s, dst_d):
            return pltpu.make_async_remote_copy(
                src_ref=src, dst_ref=dst, send_sem=send, recv_sem=recv, device_id=at(dst_s, dst_d))

        load_w = pltpu.make_async_copy(w_hbm, w.at[e], load_sem.at[0])
        load_t = pltpu.make_async_copy(table_hbm, table, load_sem.at[1])
        load_i = pltpu.make_async_copy(times_hbm, times, load_sem.at[2])
        load_w.start()
        load_t.start()
        load_i.start()

        barrier = pltpu.get_barrier_semaphore()

        def greet(k, _):
            to = lax.rem(d + k, replicas)
            pl.semaphore_signal(barrier, inc=1, device_id=at(s, to))
            pl.semaphore_signal(barrier, inc=1, device_id=at(mate, to))
            return None

        pl.semaphore_signal(barrier, inc=1, device_id=at(mate, d))
        lax.fori_loop(1, replicas, greet, None)
        relations = [
            (pair < half - 1, jnp.minimum(s + 2, sections - 1)),
            (pair > 0, jnp.maximum(s - 2, 0)),
            ((e == 1) & (s < pair_from), jnp.minimum(s + 1, sections - 1)),
            ((e == 0) & (s > 0) & (s <= pair_from), jnp.maximum(s - 1, 0)),
            (s >= 0, 2 * (half - 1 - pair) + e),
            ((s < pair_from) | (s >= sections - pair_from), sections - 1 - s),
            (line == line_len - 1, jnp.maximum(s - line_len + 1, 0)),
            (line == 0, jnp.minimum(s + line_len - 1, sections - 1)),
        ]
        expected = 2 * replicas - 1
        for wanted, other in relations:
            expected = expected + jnp.where(wanted, 1, 0)

            @pl.when(wanted)
            def _():
                pl.semaphore_signal(barrier, inc=1, device_id=at(other, d))

        @pl.when(s == 0)
        def _():
            load = pltpu.make_async_copy(lat_ref, inbox, in_sem)
            load.start()
            load.wait()

        @pl.when(pair == half - 1)
        def _():
            load = pltpu.make_async_copy(cot_ref.at[e], gin.at[0], in_sem)
            load.start()
            load.wait()

        @pl.when(s < half + 2)
        def _():
            skip[0] = jnp.zeros_like(skip[0])

        @pl.when(s < half)
        def _():
            skip[1] = jnp.zeros_like(skip[1])

        @pl.when(s >= half)
        def _():
            dskip[0] = jnp.zeros_like(dskip[0])

        @pl.when(s >= half - 2)
        def _():
            dskip[1] = jnp.zeros_like(dskip[1])

        load_w.wait()
        load_t.wait()
        load_i.wait()
        pl.semaphore_wait(barrier, expected)

        def rows(start, count):
            return pl.ds(pl.multiple_of(start, 16), count)

        core_rows = taps // 2
        piece_v = core_rows // 8 // 16 * 16
        piece_u = core_rows // 4 - piece_v
        odd = lax.rem(x, 2)
        base_v = core * core_rows + 4 * piece_u
        sibling = replica(x, zh, 1 - core)

        def u_row(parity, k):
            return core * core_rows + (2 * parity + k) * piece_u

        def v_row(px):
            return base_v + px * piece_v

        def along(k):
            return replica(lax.rem(x + k, xs), zh, core)

        def z_piece(k):
            return v_row(x) if k == 0 else u_row(odd, k - 1)

        def copy_z(slot, k):
            ref = w.at[slot, rows(z_piece(k), piece_u if k else piece_v)]
            return remote(ref, ref, z_send.at[k], z_recv.at[k], mate, d)

        def copy_v(k, px):
            ref = w.at[1 - e, rows(v_row(px), piece_v)]
            return remote(ref, ref, x_send.at[k], x_recv.at[k], s, along(k))

        def copy_u(k, parity):
            ref = w.at[1 - e, rows(u_row(parity, k), piece_u)]
            return remote(ref, ref, x_send.at[xs + k], x_recv.at[xs + k], s, along(1 if k == 0 else xs - 1))

        def copy_y(k, c):
            ref = w.at[1 - e, rows(c * core_rows + k * 4 * piece_u, 4 * (piece_v if k else piece_u))]
            return remote(ref, ref, y_send.at[k], y_recv.at[k], s, sibling)

        def share_weights():
            for k in range(3):
                copy_z(e, k).start()

        def spread_weights():
            copy_z(1 - e, 0).wait_recv()
            for k in range(1, xs):
                copy_v(k, x).start()
            for k in range(2):
                copy_z(1 - e, 1 + k).wait_recv()
                copy_u(k, odd).start()
            for k in range(1, xs):
                copy_v(k, lax.rem(x + xs - k, xs)).wait_recv()
            copy_y(1, core).start()
            for k in range(2):
                copy_u(k, 1 - odd).wait_recv()
            copy_y(0, core).start()
            for k in range(2):
                copy_y(k, 1 - core).wait_recv()

        def turn_weights(slot):
            def turn(t, _):
                src = pl.multiple_of(t * chans, chans)
                dst = pl.multiple_of((8 - t) * chans, chans)
                for r in range(0, chans, 128):
                    block = w[slot, pl.ds(src + r, 128), :]
                    wt[slot, pl.ds(dst, chans), r : r + 128] = block.T
                return None

            lax.fori_loop(0, 9, turn, None)

        @pl.when(s >= pair_from)
        def _():
            share_weights()

        @pl.when(s >= line_len)
        def _():
            turn_weights(e)

        @pl.when(s >= pair_from)
        def _():
            spread_weights()

        @pl.when(top_line)
        def _():
            turn_weights(1 - e)

        def put(t, v):
            lhs[:, t * chans : (t + 1) * chans] = v

        def slot_and_micro(i):
            return jnp.where(hop, e, i), jnp.where(hop, i, e)

        def mirror(level, micro):
            return 2 * ((sections - 1 - level) // 2) + micro

        def sends_f(i):
            return hop | ((i == 1) & (pair < half - 1))

        def copy_f(i):
            to = jnp.where(hop, jnp.where(s == pair_from - 1, pair_from + i, s + 1), jnp.minimum(s + 2, sections - 1))
            slot = jnp.where(s < pair_from - 1, i, 0)
            return remote(fout.at[i], inbox.at[slot], f_send.at[i], f_recv.at[slot], to, d)

        def wait_f(i):
            remote(fout.at[i], inbox.at[i], f_send.at[i], f_recv.at[i], mate, d).wait_recv()

        def copy_s(i):
            slot, micro = slot_and_micro(i)
            return remote(
                sout.at[i], skip.at[1 - slot], s_send.at[i], s_recv.at[1 - slot], mirror(2 * pair + slot, micro), d)

        def wait_s(slot):
            remote(sout.at[0], skip.at[slot], s_send.at[0], s_recv.at[slot], mate, d).wait_recv()

        def sends_t(i):
            return hop & (i != e)

        def copy_t(slot):
            return remote(state.at[2], state.at[slot], t_send, t_recv, mate, d)

        def copy_n(micro):
            return remote(
                nstage, gathered.at[place, rows(micro * PIX, PIX)], n_send, n_recv, mate, d)

        def forward(i, _):
            slot, micro = slot_and_micro(i)
            level = 2 * pair + slot

            @pl.when(jnp.where(hop, jnp.where(s > 0, 1, 0), 1 - i) == 1)
            def _():
                wait_f(i)

            @pl.when(level > half)
            def _():
                wait_s(slot)

            value = inbox[i].astype(jnp.float32) + skip[slot].astype(jnp.float32)
            inv_rms = lax.rsqrt(jnp.mean(value * value, axis=-1, keepdims=True) + EPS)
            norm = value * inv_rms
            gather_taps(norm, put)
            step = times[micro, 0]
            emb = table[pl.ds(step, 1), :]
            saved = jnp.where(hop, jnp.where(i == e, e, 2), i)
            for a, b in column_blocks(chans):
                pre = jnp.dot(lhs[...], w[slot, :, a:b], preferred_element_type=jnp.float32) + emb[:, a:b]
                sig = jax.nn.sigmoid(pre)
                branch = pre * sig
                result = value[:, a:b] + branch
                branch_b = branch.astype(jnp.bfloat16)
                result = result.astype(jnp.bfloat16).astype(jnp.float32)
                result = result + jnp.where(level == half - 1, branch_b.astype(jnp.float32), 0.0)
                fout[i, :, a:b] = result.astype(jnp.bfloat16)
                sout[i, :, a:b] = branch_b
                state[saved, :, chans + a : chans + b] = sig * (1.0 + pre * (1.0 - sig))

            @pl.when(sends_f(i))
            def _():
                copy_f(i).start()

            @pl.when(level < half - 1)
            def _():
                copy_s(i).start()

            @pl.when(jnp.logical_not(hop) & (i == 0))
            def _():
                inbox[1] = fout[0]

            state[saved, :, :chans] = norm
            state[saved, :, 2 * chans :] = jnp.broadcast_to(inv_rms, (PIX, 128))
            norm_b = norm.astype(jnp.bfloat16)

            @pl.when(hop | (i == e))
            def _():
                gathered[place, rows(micro * PIX, PIX), :] = norm_b

            @pl.when(jnp.logical_not(hop) & (i != e))
            def _():
                nstage[...] = norm_b
                copy_n(e).start()

            @pl.when(sends_t(i))
            def _():
                copy_t(e).start()

            return None

        lax.fori_loop(0, 2, forward, None)

        @pl.when(jnp.logical_not(top_line) & (line == line_len - 1))
        def _():
            for k in range(1, line_len):
                pl.semaphore_signal(go, inc=1, device_id=at(s - k, d))

        @pl.when(s < line_len)
        def _():
            turn_weights(e)

        @pl.when(jnp.logical_not(top_line) & (line < line_len - 1))
        def _():
            pl.semaphore_wait(go, 1)

        @pl.when(hop)
        def _():
            share_weights()
            spread_weights()

        @pl.when(jnp.logical_not(top_line))
        def _():
            turn_weights(1 - e)

        group = replicas // 2

        def copy_a(pz):
            ref = gathered.at[core * group + x * 2 + pz]
            return remote(ref, ref, a_send, a_recv, s, replica(x, 1 - zh, core))

        def copy_b(k, px):
            ref = gathered.at[pl.ds(core * group + px * 2, 2)]
            return remote(
                ref, ref, b_send.at[k - 1], b_recv.at[k - 1], s, replica(lax.rem(x + k, xs), zh, core))

        def copy_c(c):
            ref = gathered.at[pl.ds(c * group, group)]
            return remote(ref, ref, c_send, c_recv, s, sibling)

        def gather_all():
            @pl.when(jnp.logical_not(hop))
            def _():
                copy_n(1 - e).wait_recv()

            copy_a(zh).start()
            copy_a(1 - zh).wait_recv()
            for k in range(1, xs):
                copy_b(k, x).start()
            for k in range(1, xs):
                copy_b(k, lax.rem(x + xs - k, xs)).wait_recv()
            copy_c(core).start()
            copy_c(1 - core).wait_recv()
            copy_a(zh).wait_send()
            for k in range(1, xs):
                copy_b(k, x).wait_send()
            copy_c(core).wait_send()

        soon = jnp.logical_not(top_line)

        @pl.when(soon)
        def _():
            gather_all()

        @pl.when(hop)
        def _():
            copy_t(1 - e).wait_recv()

        def copy_g():
            return remote(gout.at[1], gin.at[0], g_send, g_recv, jnp.maximum(s - 2, 0), d)

        def copy_d(i):
            return remote(
                gout.at[i], dskip.at[i], d_send.at[i], d_recv.at[i], mirror(2 * pair + 1 - i, e), d)

        def wait_d(slot):
            remote(gout.at[0], dskip.at[slot], d_send.at[0], d_recv.at[slot], mate, d).wait_recv()

        def backward(i, _):
            slot = 1 - i
            level = 2 * pair + slot

            @pl.when((i == 0) & (pair < half - 1))
            def _():
                copy_g().wait_recv()

            @pl.when(level < half - 1)
            def _():
                wait_d(slot)

            grad = gin[i].astype(jnp.float32)
            factor = jnp.where(level == half - 1, 2.0, 1.0).astype(jnp.float32)
            branch_grad = grad * factor + dskip[slot].astype(jnp.float32)
            grad_pre = (branch_grad * state[slot, :, chans : 2 * chans]).astype(jnp.bfloat16).astype(jnp.float32)
            gpre[slot] = grad_pre

            @pl.when(level > 0)
            def _():
                gather_taps(grad_pre, put)
                parts = [
                    jnp.dot(lhs[...], wt[slot, :, a:b], preferred_element_type=jnp.float32)
                    for a, b in column_blocks(chans)
                ]
                gn = jnp.concatenate(parts, axis=1)
                norm = state[slot, :, :chans]
                inner = jnp.mean(gn * norm, axis=-1, keepdims=True)
                inv_rms = state[slot, :, 2 * chans : 2 * chans + 1]
                gout[i] = (grad + inv_rms * (gn - norm * inner)).astype(jnp.bfloat16)

            @pl.when((i == 1) & (pair > 0))
            def _():
                copy_g().start()

            @pl.when(level > half)
            def _():
                copy_d(i).start()

            @pl.when(i == 0)
            def _():
                gin[1] = gout[0]

            return None

        lax.fori_loop(0, 2, backward, None)

        low = lax.broadcasted_iota(jnp.int32, (1, lanes), 1) < PIX
        top_rows = ROWS // 2
        pad = jnp.zeros((ROWS - share, lanes), jnp.float32)
        pad_rows = jnp.zeros((PACK_ROWS - top_rows, lanes), jnp.float32)

        def pack_level(slot):
            for r in range(0, chans, 128):
                block = gpre[slot, :, r : r + 128]
                gtrans[r : r + 128, :] = jnp.concatenate([block, block], 0).T
            for j in range(replicas):
                first = gtrans[share * j : share * j + top_rows, :]
                rest = jnp.concatenate([gtrans[share * j + top_rows : share * (j + 1), :], pad], 0)
                block = jnp.concatenate([jnp.where(low, first, rest), pad_rows], 0)
                pack[slot, j] = block.astype(jnp.bfloat16)

        def copy_p(slot, to):
            index = slot * replicas + to
            return remote(
                pack.at[slot, to], shares.at[e, place], p_send.at[index], p_recv.at[e * replicas + place],
                2 * pair + slot, to)

        def send_share(k, _):
            to = lax.rem(d + k, replicas)
            copy_p(e, to).start()
            copy_p(1 - e, to).start()
            return None

        def pack_loop(slot, _):
            pack_level(slot)
            return None

        lax.fori_loop(0, 2, pack_loop, None)
        copy_p(1 - e, d).start()
        lax.fori_loop(1, replicas, send_share, None)
        shares[e, place] = pack[e, d]

        @pl.when(jnp.logical_not(soon))
        def _():
            gather_all()

        def wait_share(micro, slot):
            remote(
                pack.at[0, 0], shares.at[micro, slot], p_send.at[0], p_recv.at[micro * replicas + slot], mate, d
            ).wait_recv()

        def wait_shares(k, _):
            slot = lax.rem(place + k, replicas)
            wait_share(0, slot)
            wait_share(1, slot)
            return None

        wait_share(1 - e, place)
        lax.fori_loop(1, replicas, wait_shares, None)

        lane = lax.broadcasted_iota(jnp.int32, (1, lanes), 1)
        row, col = (lane // SIDE) % SIDE, lane % SIDE
        keep = []
        for kh in range(3):
            for kw in range(3):
                r, c = row - (kh - 1), col - (kw - 1)
                keep.append((r >= 0) & (r < SIDE) & (c >= 0) & (c < SIDE))
        for b in range(replicas):
            one, two = (shares[m, b].astype(jnp.float32)[:top_rows] for m in range(2))
            block = jnp.concatenate(
                [jnp.where(low, one, pltpu.roll(two, PIX, 1)), jnp.where(low, pltpu.roll(one, PIX, 1), two)], 0)
            for t in range(9):
                shift = (SIDE * (t // 3 - 1) + t % 3 - 1) % lanes
                moved = pltpu.roll(block, shift, 1) if shift else block
                moved = jnp.where(keep[t], moved, 0.0)
                amat[ROWS * t : ROWS * (t + 1), lanes * b : lanes * (b + 1)] = moved.astype(jnp.bfloat16)
        rhs = gathered[...].reshape(replicas * lanes, chans)
        for a, b in column_blocks(chans):
            total = jnp.dot(amat[...], rhs[:, a:b], preferred_element_type=jnp.float32) * scale
            for t in range(9):
                out_ref[t, :, a:b] = total[ROWS * t : ROWS * t + share]

        for k in range(3):
            copy_z(e, k).wait_send()
        for k in range(1, xs):
            copy_v(k, x).wait_send()
        for k in range(2):
            copy_u(k, odd).wait_send()
            copy_y(k, core).wait_send()

        @pl.when(hop)
        def _():
            copy_t(e).wait_send()

        @pl.when(jnp.logical_not(hop))
        def _():
            copy_n(e).wait_send()

        @pl.when(pair > 0)
        def _():
            copy_g().wait_send()

        def drain(i, _):
            @pl.when(sends_f(i))
            def _():
                copy_f(i).wait_send()

            slot, micro = slot_and_micro(i)

            @pl.when(2 * pair + slot < half - 1)
            def _():
                copy_s(i).wait_send()

            @pl.when(2 * pair + 1 - i > half)
            def _():
                copy_d(i).wait_send()

            return None

        lax.fori_loop(0, 2, drain, None)

        def drain_share(k, _):
            to = lax.rem(d + k, replicas)
            copy_p(e, to).wait_send()
            copy_p(1 - e, to).wait_send()
            return None

        copy_p(1 - e, d).wait_send()
        lax.fori_loop(1, replicas, drain_share, None)

    return kernel


def on_device(latents, cotangent, conv_weight, timesteps, time_table):
    sections = lax.axis_size("section")
    replicas = lax.axis_size("dp")
    micro, samples, side_h, side_w, chans = latents.shape
    share = chans // replicas
    scale = 1.0 / math.sqrt(micro * samples * replicas * side_h * side_w)
    fields = (micro, PIX, chans)
    dma = pltpu.SemaphoreType.DMA
    anyspace = pl.BlockSpec(memory_space=pl.ANY)
    bf, f32 = jnp.bfloat16, jnp.float32
    out = pl.pallas_call(
        make_kernel(sections, replicas, chans, share, scale, PAIR_FROM),
        out_shape=jax.ShapeDtypeStruct((9, share, chans), f32),
        in_specs=[anyspace] * 5,
        out_specs=pl.BlockSpec(memory_space=pltpu.VMEM),
        scratch_shapes=[
            pltpu.SMEM(timesteps.shape, jnp.int32),
            pltpu.VMEM((2, 9 * chans, chans), bf),
            pltpu.VMEM((2, 9 * chans, chans), bf),
            pltpu.VMEM(time_table.shape, f32),
            pltpu.VMEM((PIX, 9 * chans), bf),
            pltpu.VMEM(fields, bf),
            pltpu.VMEM(fields, bf),
            pltpu.VMEM(fields, bf),
            pltpu.VMEM(fields, bf),
            pltpu.VMEM(fields, bf),
            pltpu.VMEM(fields, bf),
            pltpu.VMEM(fields, bf),
            pltpu.VMEM((3, PIX, 2 * chans + 128), f32),
            pltpu.VMEM((2, PIX, chans), f32),
            pltpu.VMEM((chans, micro * PIX), f32),
            pltpu.VMEM((2, replicas, PACK_ROWS, micro * PIX), bf),
            pltpu.VMEM((2, replicas, PACK_ROWS, micro * PIX), bf),
            pltpu.VMEM((replicas, micro * PIX, chans), bf),
            pltpu.VMEM((PIX, chans), bf),
            pltpu.VMEM((9 * ROWS, replicas * micro * PIX), bf),
            dma((3,)), dma, dma((2,)), dma((2,)), dma((2,)), dma((2,)), dma, dma, dma((2,)), dma((2,)),
            dma, dma, dma((replicas // 4 - 1,)), dma((replicas // 4 - 1,)), dma, dma,
            dma((2 * replicas,)), dma((2 * replicas,)),
            dma, dma, dma, dma, dma((3,)), dma((3,)), dma((6,)), dma((6,)), dma((2,)), dma((2,)),
            pltpu.SemaphoreType.REGULAR,
        ],
        compiler_params=pltpu.CompilerParams(
            collective_id=0, has_side_effects=True, vmem_limit_bytes=56 * 2**20
        ),
        name="levels",
    )(
        timesteps,
        latents.reshape(fields),
        cotangent.reshape(fields),
        conv_weight.reshape(9 * chans, chans),
        time_table,
    )
    return jnp.swapaxes(out, 1, 2).reshape(1, 3, 3, chans, share)


def solution(mesh):
    in_specs = (
        P(None, "dp", None, None, None),
        P(None, "dp", None, None, None),
        P("section", None, None, None, None),
        P(None, "dp"),
        P(),
    )
    out_specs = P("section", None, None, None, "dp")
    return jax.shard_map(
        on_device, mesh=mesh, in_specs=in_specs, out_specs=out_specs, check_vma=False
    )
```

```python
import math

import jax
import jax.numpy as jnp
from jax import lax
from jax.experimental import pallas as pl
from jax.experimental.pallas import tpu as pltpu
from jax.sharding import PartitionSpec as P

EPS = 1e-05
SIDE = 8
PIX = SIDE * SIDE
PAIR_FROM = 8
PACK_ROWS = 32
ROWS = 48


def gather_taps(value, store):
    chans = value.shape[1]
    col = lax.broadcasted_iota(jnp.int32, (PIX, 1), 0) % SIDE
    edge = jnp.zeros((SIDE, chans), jnp.float32)
    left = jnp.where(col > 0, pltpu.roll(value, 1, 0), 0.0)
    right = jnp.where(col < SIDE - 1, pltpu.roll(value, PIX - 1, 0), 0.0)
    for kw, v in enumerate((left, value, right)):
        store(kw, jnp.concatenate([edge, v[: PIX - SIDE]], 0).astype(jnp.bfloat16))
        store(3 + kw, v.astype(jnp.bfloat16))
        store(6 + kw, jnp.concatenate([v[SIDE:], edge], 0).astype(jnp.bfloat16))


def column_blocks(chans):
    return [(a, min(a + 256, chans)) for a in range(0, chans, 256)]


def make_kernel(sections, replicas, chans, share, scale, pair_from):
    half = sections // 2
    xs = replicas // 4
    lanes = 2 * PIX
    taps = 9 * chans

    def kernel(
        times_hbm, lat_ref, cot_ref, w_hbm, table_hbm, out_ref,
        times, w, wt, table, lhs, inbox, skip, fout, sout, gin, dskip, gout,
        state, gpre, gtrans, pack, shares, gathered, nstage, amat,
        load_sem, in_sem, f_send, f_recv, s_send, s_recv, g_send, g_recv, d_send, d_recv,
        a_send, a_recv, b_send, b_recv, c_send, c_recv, p_send, p_recv,
        n_send, n_recv, t_send, t_recv, z_send, z_recv, v_send, v_recv, u_send, u_recv, y_send, y_recv, go,
    ):
        s = lax.axis_index("section")
        d = lax.axis_index("dp")
        core = lax.rem(d, 2)
        zh = lax.rem(d // 2, 2)
        x = d // 4
        place = core * (replicas // 2) + x * 2 + zh
        pair, e = s // 2, lax.rem(s, 2)
        mate = s + 1 - 2 * e
        line_len = 4
        line = lax.rem(s, line_len)
        top_line = s >= sections - line_len
        hop = s < pair_from

        def at(dst_s, dst_d):
            return {"section": dst_s, "dp": dst_d}

        def replica(px, pz, pc):
            return px * 4 + pz * 2 + pc

        def remote(src, dst, send, recv, dst_s, dst_d):
            return pltpu.make_async_remote_copy(
                src_ref=src, dst_ref=dst, send_sem=send, recv_sem=recv, device_id=at(dst_s, dst_d))

        load_w = pltpu.make_async_copy(w_hbm, w.at[e], load_sem.at[0])
        load_t = pltpu.make_async_copy(table_hbm, table, load_sem.at[1])
        load_i = pltpu.make_async_copy(times_hbm, times, load_sem.at[2])
        load_w.start()
        load_t.start()
        load_i.start()

        barrier = pltpu.get_barrier_semaphore()

        def greet(k, _):
            to = lax.rem(d + k, replicas)
            pl.semaphore_signal(barrier, inc=1, device_id=at(s, to))
            pl.semaphore_signal(barrier, inc=1, device_id=at(mate, to))
            return None

        pl.semaphore_signal(barrier, inc=1, device_id=at(mate, d))
        lax.fori_loop(1, replicas, greet, None)
        relations = [
            (pair < half - 1, jnp.minimum(s + 2, sections - 1)),
            (pair > 0, jnp.maximum(s - 2, 0)),
            ((e == 1) & (s < pair_from), jnp.minimum(s + 1, sections - 1)),
            ((e == 0) & (s > 0) & (s <= pair_from), jnp.maximum(s - 1, 0)),
            (s >= 0, 2 * (half - 1 - pair) + e),
            ((s < pair_from) | (s >= sections - pair_from), sections - 1 - s),
            (line == line_len - 1, jnp.maximum(s - line_len + 1, 0)),
            (line == 0, jnp.minimum(s + line_len - 1, sections - 1)),
        ]
        expected = 2 * replicas - 1
        for wanted, other in relations:
            expected = expected + jnp.where(wanted, 1, 0)

            @pl.when(wanted)
            def _():
                pl.semaphore_signal(barrier, inc=1, device_id=at(other, d))

        @pl.when(s == 0)
        def _():
            load = pltpu.make_async_copy(lat_ref, inbox, in_sem)
            load.start()
            load.wait()

        @pl.when(pair == half - 1)
        def _():
            load = pltpu.make_async_copy(cot_ref.at[e], gin.at[0], in_sem)
            load.start()
            load.wait()

        @pl.when(s < half + 2)
        def _():
            skip[0] = jnp.zeros_like(skip[0])

        @pl.when(s < half)
        def _():
            skip[1] = jnp.zeros_like(skip[1])

        @pl.when(s >= half)
        def _():
            dskip[0] = jnp.zeros_like(dskip[0])

        @pl.when(s >= half - 2)
        def _():
            dskip[1] = jnp.zeros_like(dskip[1])

        pl.semaphore_wait(barrier, expected)

        def rows(start, count):
            return pl.ds(pl.multiple_of(start, 16), count)

        core_rows = taps // 2
        piece_v = core_rows // 16 // 16 * 16
        all_v = 8 * piece_v
        all_u = core_rows - all_v
        cut_u = [all_u // 2 * k // 4 // 16 * 16 for k in range(5)]
        size_u = [b - a for a, b in zip(cut_u, cut_u[1:])]
        base_v = core * core_rows + all_u
        odd = lax.rem(x, 2)
        sibling = replica(x, zh, 1 - core)

        def u_row(parity, k):
            return core * core_rows + parity * (all_u // 2) + cut_u[k]

        def v_row(px, k):
            return base_v + (2 * px + k) * piece_v

        def along(k):
            return replica(lax.rem(x + k, xs), zh, core)

        def copy_z(k):
            row, count = (v_row(x, k), piece_v) if k < 2 else (u_row(odd, k - 2), size_u[k - 2])
            return remote(
                w_hbm.at[rows(row, count)], w.at[e, rows(row, count)], z_send.at[k], z_recv.at[k], mate, d)

        def wait_z(k):
            row, count = (v_row(x, k), piece_v) if k < 2 else (u_row(odd, k - 2), size_u[k - 2])
            ref = w.at[1 - e, rows(row, count)]
            remote(ref, ref, z_send.at[k], z_recv.at[k], mate, d).wait_recv()

        def copy_v(n, k, px):
            ref = w.at[1 - e, rows(v_row(px, k), piece_v)]
            return remote(ref, ref, v_send.at[3 * k + n - 1], v_recv.at[3 * k + n - 1], s, along(n))

        def copy_u(k, parity):
            ref = w.at[1 - e, rows(u_row(parity, k), size_u[k])]
            return remote(ref, ref, u_send.at[k], u_recv.at[k], s, along(xs - 1 if k % 2 else 1))

        def copy_y(k, c):
            row, count = (c * core_rows + all_u, all_v) if k == 0 else (c * core_rows, all_u)
            ref = w.at[1 - e, rows(row, count)]
            return remote(ref, ref, y_send.at[k], y_recv.at[k], s, sibling)

        def share_weights():
            for k in range(6):
                copy_z(k).start()

        def spread_z():
            for k in range(2):
                wait_z(k)
                for n in (1, xs - 1, 2):
                    copy_v(n, k, x).start()

        def spread_x():
            for k in range(4):
                wait_z(2 + k)
                copy_u(k, odd).start()
            for k in range(2):
                for n in range(1, xs):
                    copy_v(n, k, lax.rem(x + xs - n, xs)).wait_recv()
            copy_y(0, core).start()
            for k in range(4):
                copy_u(k, 1 - odd).wait_recv()
            copy_y(1, core).start()

        def spread_y():
            for k in range(2):
                copy_y(k, 1 - core).wait_recv()

        def turn_weights(slot):
            def turn(t, _):
                src = pl.multiple_of(t * chans, chans)
                dst = pl.multiple_of((8 - t) * chans, chans)
                for r in range(0, chans, 128):
                    block = w[slot, pl.ds(src + r, 128), :]
                    wt[slot, pl.ds(dst, chans), r : r + 128] = block.T
                return None

            lax.fori_loop(0, 9, turn, None)

        @pl.when(s >= pair_from)
        def _():
            share_weights()

        load_w.wait()
        load_t.wait()
        load_i.wait()

        @pl.when(s >= line_len)
        def _():
            turn_weights(e)

        @pl.when(s >= pair_from)
        def _():
            spread_z()
            spread_x()
            spread_y()

        @pl.when(top_line)
        def _():
            turn_weights(1 - e)

        def put(t, v):
            lhs[:, t * chans : (t + 1) * chans] = v

        def slot_and_micro(i):
            return jnp.where(hop, e, i), jnp.where(hop, i, e)

        def mirror(level, micro):
            return 2 * ((sections - 1 - level) // 2) + micro

        def sends_f(i):
            return hop | ((i == 1) & (pair < half - 1))

        def copy_f(i):
            to = jnp.where(hop, jnp.where(s == pair_from - 1, pair_from + i, s + 1), jnp.minimum(s + 2, sections - 1))
            slot = jnp.where(s < pair_from - 1, i, 0)
            return remote(fout.at[i], inbox.at[slot], f_send.at[i], f_recv.at[slot], to, d)

        def wait_f(i):
            remote(fout.at[i], inbox.at[i], f_send.at[i], f_recv.at[i], mate, d).wait_recv()

        def copy_s(i):
            slot, micro = slot_and_micro(i)
            return remote(
                sout.at[i], skip.at[1 - slot], s_send.at[i], s_recv.at[1 - slot], mirror(2 * pair + slot, micro), d)

        def wait_s(slot):
            remote(sout.at[0], skip.at[slot], s_send.at[0], s_recv.at[slot], mate, d).wait_recv()

        def sends_t(i):
            return hop & (i != e)

        def copy_t(slot):
            return remote(state.at[2], state.at[slot], t_send, t_recv, mate, d)

        def copy_n(micro):
            return remote(
                nstage, gathered.at[place, rows(micro * PIX, PIX)], n_send, n_recv, mate, d)

        def forward(i, _):
            slot, micro = slot_and_micro(i)
            level = 2 * pair + slot

            @pl.when(jnp.where(hop, jnp.where(s > 0, 1, 0), 1 - i) == 1)
            def _():
                wait_f(i)

            @pl.when(level > half)
            def _():
                wait_s(slot)

            value = inbox[i].astype(jnp.float32) + skip[slot].astype(jnp.float32)
            inv_rms = lax.rsqrt(jnp.mean(value * value, axis=-1, keepdims=True) + EPS)
            norm = value * inv_rms
            gather_taps(norm, put)
            step = times[micro, 0]
            emb = table[pl.ds(step, 1), :]
            saved = jnp.where(hop, jnp.where(i == e, e, 2), i)
            for a, b in column_blocks(chans):
                pre = jnp.dot(lhs[...], w[slot, :, a:b], preferred_element_type=jnp.float32) + emb[:, a:b]
                sig = jax.nn.sigmoid(pre)
                branch = pre * sig
                result = value[:, a:b] + branch
                branch_b = branch.astype(jnp.bfloat16)
                result = result.astype(jnp.bfloat16).astype(jnp.float32)
                result = result + jnp.where(level == half - 1, branch_b.astype(jnp.float32), 0.0)
                fout[i, :, a:b] = result.astype(jnp.bfloat16)
                sout[i, :, a:b] = branch_b
                state[saved, :, chans + a : chans + b] = sig * (1.0 + pre * (1.0 - sig))

            @pl.when(sends_f(i))
            def _():
                copy_f(i).start()

            @pl.when(level < half - 1)
            def _():
                copy_s(i).start()

            @pl.when(jnp.logical_not(hop) & (i == 0))
            def _():
                inbox[1] = fout[0]

            state[saved, :, :chans] = norm
            state[saved, :, 2 * chans :] = jnp.broadcast_to(inv_rms, (PIX, 128))
            norm_b = norm.astype(jnp.bfloat16)

            @pl.when(hop | (i == e))
            def _():
                gathered[place, rows(micro * PIX, PIX), :] = norm_b

            @pl.when(jnp.logical_not(hop) & (i != e))
            def _():
                nstage[...] = norm_b
                copy_n(e).start()

            @pl.when(sends_t(i))
            def _():
                copy_t(e).start()

            return None

        lax.fori_loop(0, 2, forward, None)

        @pl.when(jnp.logical_not(top_line) & (line == line_len - 1))
        def _():
            for k in range(1, line_len):
                pl.semaphore_signal(go, inc=1, device_id=at(s - k, d))

        @pl.when(s < line_len)
        def _():
            turn_weights(e)

        @pl.when(jnp.logical_not(top_line) & (line < line_len - 1))
        def _():
            pl.semaphore_wait(go, 1)

        group = replicas // 2

        def copy_a(pz):
            ref = gathered.at[core * group + x * 2 + pz]
            return remote(ref, ref, a_send, a_recv, s, replica(x, 1 - zh, core))

        def copy_b(k, px):
            ref = gathered.at[pl.ds(core * group + px * 2, 2)]
            return remote(
                ref, ref, b_send.at[k - 1], b_recv.at[k - 1], s, replica(lax.rem(x + k, xs), zh, core))

        def copy_c(c):
            ref = gathered.at[pl.ds(c * group, group)]
            return remote(ref, ref, c_send, c_recv, s, sibling)

        def gather_a():
            copy_a(zh).start()

        def gather_b():
            copy_a(1 - zh).wait_recv()
            for k in range(1, xs):
                copy_b(k, x).start()

        def gather_c():
            for k in range(1, xs):
                copy_b(k, lax.rem(x + xs - k, xs)).wait_recv()
            copy_c(core).start()
            copy_c(1 - core).wait_recv()

        def gather_all():
            copy_n(1 - e).wait_recv()
            gather_a()
            gather_b()
            gather_c()

        @pl.when(hop)
        def _():
            share_weights()
            gather_a()
            spread_z()
            gather_b()
            spread_x()
            gather_c()
            spread_y()

        @pl.when(jnp.logical_not(top_line))
        def _():
            turn_weights(1 - e)

        soon = jnp.logical_not(top_line)

        @pl.when(soon & jnp.logical_not(hop))
        def _():
            gather_all()

        @pl.when(hop)
        def _():
            copy_t(1 - e).wait_recv()

        low = lax.broadcasted_iota(jnp.int32, (1, lanes), 1) < PIX
        top_rows = ROWS // 2
        pad = jnp.zeros((ROWS - share, lanes), jnp.float32)
        pad_rows = jnp.zeros((PACK_ROWS - top_rows, lanes), jnp.float32)

        def pack_level(slot):
            for r in range(0, chans, 128):
                block = gpre[slot, :, r : r + 128]
                gtrans[r : r + 128, :] = jnp.concatenate([block, block], 0).T
            for j in range(replicas):
                first = gtrans[share * j : share * j + top_rows, :]
                rest = jnp.concatenate([gtrans[share * j + top_rows : share * (j + 1), :], pad], 0)
                block = jnp.concatenate([jnp.where(low, first, rest), pad_rows], 0)
                pack[slot, j] = block.astype(jnp.bfloat16)

        def copy_p(slot, to):
            index = slot * replicas + to
            return remote(
                pack.at[slot, to], shares.at[e, place], p_send.at[index], p_recv.at[e * replicas + place],
                2 * pair + slot, to)

        def send_level(slot):
            pack_level(slot)

            def send_share(k, _):
                copy_p(slot, lax.rem(d + k, replicas)).start()
                return None

            lax.fori_loop(jnp.where(slot == e, 1, 0), replicas, send_share, None)

        def copy_g():
            return remote(gout.at[1], gin.at[0], g_send, g_recv, jnp.maximum(s - 2, 0), d)

        def copy_d(i):
            return remote(
                gout.at[i], dskip.at[i], d_send.at[i], d_recv.at[i], mirror(2 * pair + 1 - i, e), d)

        def wait_d(slot):
            remote(gout.at[0], dskip.at[slot], d_send.at[0], d_recv.at[slot], mate, d).wait_recv()

        def backward(i, _):
            slot = 1 - i
            level = 2 * pair + slot

            @pl.when((i == 0) & (pair < half - 1))
            def _():
                copy_g().wait_recv()

            @pl.when(level < half - 1)
            def _():
                wait_d(slot)

            grad = gin[i].astype(jnp.float32)
            factor = jnp.where(level == half - 1, 2.0, 1.0).astype(jnp.float32)
            branch_grad = grad * factor + dskip[slot].astype(jnp.float32)
            grad_pre = (branch_grad * state[slot, :, chans : 2 * chans]).astype(jnp.bfloat16).astype(jnp.float32)
            gpre[slot] = grad_pre

            @pl.when(level == 1)
            def _():
                send_level(1)

            @pl.when(level > 0)
            def _():
                gather_taps(grad_pre, put)
                parts = [
                    jnp.dot(lhs[...], wt[slot, :, a:b], preferred_element_type=jnp.float32)
                    for a, b in column_blocks(chans)
                ]
                gn = jnp.concatenate(parts, axis=1)
                norm = state[slot, :, :chans]
                inner = jnp.mean(gn * norm, axis=-1, keepdims=True)
                inv_rms = state[slot, :, 2 * chans : 2 * chans + 1]
                gout[i] = (grad + inv_rms * (gn - norm * inner)).astype(jnp.bfloat16)

            @pl.when((i == 1) & (pair > 0))
            def _():
                copy_g().start()

            @pl.when(level > half)
            def _():
                copy_d(i).start()

            @pl.when(i == 0)
            def _():
                gin[1] = gout[0]

            return None

        lax.fori_loop(0, 2, backward, None)

        @pl.when(pair > 0)
        def _():
            send_level(1)

        send_level(0)
        shares[e, place] = pack[e, d]

        @pl.when(jnp.logical_not(soon))
        def _():
            gather_all()

        def wait_share(micro, slot):
            remote(
                pack.at[0, 0], shares.at[micro, slot], p_send.at[0], p_recv.at[micro * replicas + slot], mate, d
            ).wait_recv()

        def wait_shares(k, _):
            slot = lax.rem(place + k, replicas)
            wait_share(0, slot)
            wait_share(1, slot)
            return None

        wait_share(1 - e, place)
        lax.fori_loop(1, replicas, wait_shares, None)

        lane = lax.broadcasted_iota(jnp.int32, (1, lanes), 1)
        row, col = (lane // SIDE) % SIDE, lane % SIDE
        keep = []
        for kh in range(3):
            for kw in range(3):
                r, c = row - (kh - 1), col - (kw - 1)
                keep.append((r >= 0) & (r < SIDE) & (c >= 0) & (c < SIDE))
        for b in range(replicas):
            one, two = (shares[m, b].astype(jnp.float32)[:top_rows] for m in range(2))
            block = jnp.concatenate(
                [jnp.where(low, one, pltpu.roll(two, PIX, 1)), jnp.where(low, pltpu.roll(one, PIX, 1), two)], 0)
            for t in range(9):
                shift = (SIDE * (t // 3 - 1) + t % 3 - 1) % lanes
                moved = pltpu.roll(block, shift, 1) if shift else block
                moved = jnp.where(keep[t], moved, 0.0)
                amat[ROWS * t : ROWS * (t + 1), lanes * b : lanes * (b + 1)] = moved.astype(jnp.bfloat16)
        rhs = gathered[...].reshape(replicas * lanes, chans)
        for a, b in column_blocks(chans):
            total = jnp.dot(amat[...], rhs[:, a:b], preferred_element_type=jnp.float32) * scale
            for t in range(9):
                out_ref[t, :, a:b] = total[ROWS * t : ROWS * t + share]

        copy_a(zh).wait_send()
        for k in range(1, xs):
            copy_b(k, x).wait_send()
        copy_c(core).wait_send()
        for k in range(6):
            copy_z(k).wait_send()
        for k in range(2):
            for n in range(1, xs):
                copy_v(n, k, x).wait_send()
            copy_y(k, core).wait_send()
        for k in range(4):
            copy_u(k, odd).wait_send()

        @pl.when(hop)
        def _():
            copy_t(e).wait_send()

        @pl.when(jnp.logical_not(hop))
        def _():
            copy_n(e).wait_send()

        @pl.when(pair > 0)
        def _():
            copy_g().wait_send()

        def drain(i, _):
            @pl.when(sends_f(i))
            def _():
                copy_f(i).wait_send()

            slot, micro = slot_and_micro(i)

            @pl.when(2 * pair + slot < half - 1)
            def _():
                copy_s(i).wait_send()

            @pl.when(2 * pair + 1 - i > half)
            def _():
                copy_d(i).wait_send()

            return None

        lax.fori_loop(0, 2, drain, None)

        def drain_share(k, _):
            to = lax.rem(d + k, replicas)
            copy_p(e, to).wait_send()
            copy_p(1 - e, to).wait_send()
            return None

        copy_p(1 - e, d).wait_send()
        lax.fori_loop(1, replicas, drain_share, None)

    return kernel


def on_device(latents, cotangent, conv_weight, timesteps, time_table):
    sections = lax.axis_size("section")
    replicas = lax.axis_size("dp")
    micro, samples, side_h, side_w, chans = latents.shape
    share = chans // replicas
    scale = 1.0 / math.sqrt(micro * samples * replicas * side_h * side_w)
    fields = (micro, PIX, chans)
    dma = pltpu.SemaphoreType.DMA
    anyspace = pl.BlockSpec(memory_space=pl.ANY)
    bf, f32 = jnp.bfloat16, jnp.float32
    out = pl.pallas_call(
        make_kernel(sections, replicas, chans, share, scale, PAIR_FROM),
        out_shape=jax.ShapeDtypeStruct((9, share, chans), f32),
        in_specs=[anyspace] * 5,
        out_specs=pl.BlockSpec(memory_space=pltpu.VMEM),
        scratch_shapes=[
            pltpu.SMEM(timesteps.shape, jnp.int32),
            pltpu.VMEM((2, 9 * chans, chans), bf),
            pltpu.VMEM((2, 9 * chans, chans), bf),
            pltpu.VMEM(time_table.shape, f32),
            pltpu.VMEM((PIX, 9 * chans), bf),
            pltpu.VMEM(fields, bf),
            pltpu.VMEM(fields, bf),
            pltpu.VMEM(fields, bf),
            pltpu.VMEM(fields, bf),
            pltpu.VMEM(fields, bf),
            pltpu.VMEM(fields, bf),
            pltpu.VMEM(fields, bf),
            pltpu.VMEM((3, PIX, 2 * chans + 128), f32),
            pltpu.VMEM((2, PIX, chans), f32),
            pltpu.VMEM((chans, micro * PIX), f32),
            pltpu.VMEM((2, replicas, PACK_ROWS, micro * PIX), bf),
            pltpu.VMEM((2, replicas, PACK_ROWS, micro * PIX), bf),
            pltpu.VMEM((replicas, micro * PIX, chans), bf),
            pltpu.VMEM((PIX, chans), bf),
            pltpu.VMEM((9 * ROWS, replicas * micro * PIX), bf),
            dma((3,)), dma, dma((2,)), dma((2,)), dma((2,)), dma((2,)), dma, dma, dma((2,)), dma((2,)),
            dma, dma, dma((replicas // 4 - 1,)), dma((replicas // 4 - 1,)), dma, dma,
            dma((2 * replicas,)), dma((2 * replicas,)),
            dma, dma, dma, dma, dma((6,)), dma((6,)), dma((6,)), dma((6,)), dma((4,)), dma((4,)), dma((2,)), dma((2,)),
            pltpu.SemaphoreType.REGULAR,
        ],
        compiler_params=pltpu.CompilerParams(
            collective_id=0, has_side_effects=True, vmem_limit_bytes=56 * 2**20
        ),
        name="levels",
    )(
        timesteps,
        latents.reshape(fields),
        cotangent.reshape(fields),
        conv_weight.reshape(9 * chans, chans),
        time_table,
    )
    return jnp.swapaxes(out, 1, 2).reshape(1, 3, 3, chans, share)


def solution(mesh):
    in_specs = (
        P(None, "dp", None, None, None),
        P(None, "dp", None, None, None),
        P("section", None, None, None, None),
        P(None, "dp"),
        P(),
    )
    out_specs = P("section", None, None, None, "dp")
    return jax.shard_map(
        on_device, mesh=mesh, in_specs=in_specs, out_specs=out_specs, check_vma=False
    )
```

```python
import math

import jax
import jax.numpy as jnp
from jax import lax
from jax.experimental import pallas as pl
from jax.experimental.pallas import tpu as pltpu
from jax.sharding import PartitionSpec as P

EPS = 1e-05
SIDE = 8
PIX = SIDE * SIDE
PAIR_FROM = 8
PACK_ROWS = 32
ROWS = 48


def gather_taps(value, store):
    chans = value.shape[1]
    col = lax.broadcasted_iota(jnp.int32, (PIX, 1), 0) % SIDE
    edge = jnp.zeros((SIDE, chans), jnp.float32)
    left = jnp.where(col > 0, pltpu.roll(value, 1, 0), 0.0)
    right = jnp.where(col < SIDE - 1, pltpu.roll(value, PIX - 1, 0), 0.0)
    for kw, v in enumerate((left, value, right)):
        store(kw, jnp.concatenate([edge, v[: PIX - SIDE]], 0).astype(jnp.bfloat16))
        store(3 + kw, v.astype(jnp.bfloat16))
        store(6 + kw, jnp.concatenate([v[SIDE:], edge], 0).astype(jnp.bfloat16))


def column_blocks(chans):
    return [(a, min(a + 256, chans)) for a in range(0, chans, 256)]


def make_kernel(sections, replicas, chans, share, scale, pair_from):
    half = sections // 2
    xs = replicas // 4
    lanes = 2 * PIX
    taps = 9 * chans

    def kernel(
        times_hbm, lat_ref, cot_ref, w_hbm, table_hbm, out_ref,
        times, w, wt, table, lhs, inbox, skip, fout, sout, gin, dskip, gout,
        state, gpre, gtrans, pack, shares, gathered, nstage, amat,
        load_sem, in_sem, f_send, f_recv, s_send, s_recv, g_send, g_recv, d_send, d_recv,
        a_send, a_recv, b_send, b_recv, c_send, c_recv, p_send, p_recv,
        n_send, n_recv, t_send, t_recv, z_send, z_recv, v_send, v_recv, u_send, u_recv, y_send, y_recv, go,
    ):
        s = lax.axis_index("section")
        d = lax.axis_index("dp")
        core = lax.rem(d, 2)
        zh = lax.rem(d // 2, 2)
        x = d // 4
        place = core * (replicas // 2) + x * 2 + zh
        pair, e = s // 2, lax.rem(s, 2)
        mate = s + 1 - 2 * e
        line_len = 4
        line = lax.rem(s, line_len)
        top_line = s >= sections - line_len
        hop = s < pair_from

        def at(dst_s, dst_d):
            return {"section": dst_s, "dp": dst_d}

        def replica(px, pz, pc):
            return px * 4 + pz * 2 + pc

        def remote(src, dst, send, recv, dst_s, dst_d):
            return pltpu.make_async_remote_copy(
                src_ref=src, dst_ref=dst, send_sem=send, recv_sem=recv, device_id=at(dst_s, dst_d))

        load_w = pltpu.make_async_copy(w_hbm, w.at[e], load_sem.at[0])
        load_t = pltpu.make_async_copy(table_hbm, table, load_sem.at[1])
        load_i = pltpu.make_async_copy(times_hbm, times, load_sem.at[2])
        load_w.start()
        load_t.start()
        load_i.start()

        barrier = pltpu.get_barrier_semaphore()

        def greet(k, _):
            to = lax.rem(d + k, replicas)
            pl.semaphore_signal(barrier, inc=1, device_id=at(s, to))
            pl.semaphore_signal(barrier, inc=1, device_id=at(mate, to))
            return None

        pl.semaphore_signal(barrier, inc=1, device_id=at(mate, d))
        lax.fori_loop(1, replicas, greet, None)
        relations = [
            (pair < half - 1, jnp.minimum(s + 2, sections - 1)),
            (pair > 0, jnp.maximum(s - 2, 0)),
            ((e == 1) & (s < pair_from), jnp.minimum(s + 1, sections - 1)),
            ((e == 0) & (s > 0) & (s <= pair_from), jnp.maximum(s - 1, 0)),
            (s >= 0, 2 * (half - 1 - pair) + e),
            ((s < pair_from) | (s >= sections - pair_from), sections - 1 - s),
            (line == line_len - 1, jnp.maximum(s - line_len + 1, 0)),
            (line == 0, jnp.minimum(s + line_len - 1, sections - 1)),
        ]
        expected = 2 * replicas - 1
        for wanted, other in relations:
            expected = expected + jnp.where(wanted, 1, 0)

            @pl.when(wanted)
            def _():
                pl.semaphore_signal(barrier, inc=1, device_id=at(other, d))

        @pl.when(s == 0)
        def _():
            load = pltpu.make_async_copy(lat_ref, inbox, in_sem)
            load.start()
            load.wait()

        @pl.when(pair == half - 1)
        def _():
            load = pltpu.make_async_copy(cot_ref.at[e], gin.at[0], in_sem)
            load.start()
            load.wait()

        @pl.when(s < half + 2)
        def _():
            skip[0] = jnp.zeros_like(skip[0])

        @pl.when(s < half)
        def _():
            skip[1] = jnp.zeros_like(skip[1])

        @pl.when(s >= half)
        def _():
            dskip[0] = jnp.zeros_like(dskip[0])

        @pl.when(s >= half - 2)
        def _():
            dskip[1] = jnp.zeros_like(dskip[1])

        pl.semaphore_wait(barrier, expected)

        def rows(start, count):
            return pl.ds(pl.multiple_of(start, 16), count)

        core_rows = taps // 2
        piece_v = core_rows // 16 // 16 * 16
        all_v = 8 * piece_v
        all_u = core_rows - all_v
        cut_u = [all_u // 2 * k // 4 // 16 * 16 for k in range(5)]
        size_u = [b - a for a, b in zip(cut_u, cut_u[1:])]
        base_v = core * core_rows + all_u
        odd = lax.rem(x, 2)
        sibling = replica(x, zh, 1 - core)

        def u_row(parity, k):
            return core * core_rows + parity * (all_u // 2) + cut_u[k]

        def v_row(px, k):
            return base_v + (2 * px + k) * piece_v

        def along(k):
            return replica(lax.rem(x + k, xs), zh, core)

        def copy_z(k):
            row, count = (v_row(x, k), piece_v) if k < 2 else (u_row(odd, k - 2), size_u[k - 2])
            return remote(
                w_hbm.at[rows(row, count)], w.at[e, rows(row, count)], z_send.at[k], z_recv.at[k], mate, d)

        def wait_z(k):
            row, count = (v_row(x, k), piece_v) if k < 2 else (u_row(odd, k - 2), size_u[k - 2])
            ref = w.at[1 - e, rows(row, count)]
            remote(ref, ref, z_send.at[k], z_recv.at[k], mate, d).wait_recv()

        def copy_v(n, k, px):
            ref = w.at[1 - e, rows(v_row(px, k), piece_v)]
            return remote(ref, ref, v_send.at[3 * k + n - 1], v_recv.at[3 * k + n - 1], s, along(n))

        def copy_u(k, parity):
            ref = w.at[1 - e, rows(u_row(parity, k), size_u[k])]
            return remote(ref, ref, u_send.at[k], u_recv.at[k], s, along(xs - 1 if k % 2 else 1))

        def copy_y(k, c):
            row, count = (c * core_rows + all_u, all_v) if k == 0 else (c * core_rows, all_u)
            ref = w.at[1 - e, rows(row, count)]
            return remote(ref, ref, y_send.at[k], y_recv.at[k], s, sibling)

        def share_weights():
            for k in range(6):
                copy_z(k).start()

        def spread_z():
            for k in range(2):
                wait_z(k)
                for n in (1, xs - 1, 2):
                    copy_v(n, k, x).start()

        def spread_x():
            for k in range(4):
                wait_z(2 + k)
                copy_u(k, odd).start()
            for k in range(2):
                for n in range(1, xs):
                    copy_v(n, k, lax.rem(x + xs - n, xs)).wait_recv()
            copy_y(0, core).start()
            for k in range(4):
                copy_u(k, 1 - odd).wait_recv()
            copy_y(1, core).start()

        def spread_y():
            for k in range(2):
                copy_y(k, 1 - core).wait_recv()

        def turn_weights(slot):
            def turn(t, _):
                src = pl.multiple_of(t * chans, chans)
                dst = pl.multiple_of((8 - t) * chans, chans)
                for r in range(0, chans, 128):
                    block = w[slot, pl.ds(src + r, 128), :]
                    wt[slot, pl.ds(dst, chans), r : r + 128] = block.T
                return None

            lax.fori_loop(0, 9, turn, None)

        @pl.when(s >= pair_from)
        def _():
            share_weights()

        load_w.wait()
        load_t.wait()
        load_i.wait()

        @pl.when(s >= line_len)
        def _():
            turn_weights(e)

        @pl.when(s >= pair_from)
        def _():
            spread_z()
            spread_x()
            spread_y()

        @pl.when(top_line)
        def _():
            turn_weights(1 - e)

        def put(t, v):
            lhs[:, t * chans : (t + 1) * chans] = v

        def slot_and_micro(i):
            return jnp.where(hop, e, i), jnp.where(hop, i, e)

        def mirror(level, micro):
            return 2 * ((sections - 1 - level) // 2) + micro

        def sends_f(i):
            return hop | ((i == 1) & (pair < half - 1))

        def copy_f(i):
            to = jnp.where(hop, jnp.where(s == pair_from - 1, pair_from + i, s + 1), jnp.minimum(s + 2, sections - 1))
            slot = jnp.where(s < pair_from - 1, i, 0)
            return remote(fout.at[i], inbox.at[slot], f_send.at[i], f_recv.at[slot], to, d)

        def wait_f(i):
            remote(fout.at[i], inbox.at[i], f_send.at[i], f_recv.at[i], mate, d).wait_recv()

        def copy_s(i):
            slot, micro = slot_and_micro(i)
            return remote(
                sout.at[i], skip.at[1 - slot], s_send.at[i], s_recv.at[1 - slot], mirror(2 * pair + slot, micro), d)

        def wait_s(slot):
            remote(sout.at[0], skip.at[slot], s_send.at[0], s_recv.at[slot], mate, d).wait_recv()

        def sends_t(i):
            return hop & (i != e)

        def copy_t(slot):
            return remote(state.at[2], state.at[slot], t_send, t_recv, mate, d)

        def copy_n(micro):
            return remote(
                nstage, gathered.at[place, rows(micro * PIX, PIX)], n_send, n_recv, mate, d)

        def forward(i, _):
            slot, micro = slot_and_micro(i)
            level = 2 * pair + slot

            @pl.when(jnp.where(hop, jnp.where(s > 0, 1, 0), 1 - i) == 1)
            def _():
                wait_f(i)

            @pl.when(level > half)
            def _():
                wait_s(slot)

            value = inbox[i].astype(jnp.float32) + skip[slot].astype(jnp.float32)
            inv_rms = lax.rsqrt(jnp.mean(value * value, axis=-1, keepdims=True) + EPS)
            norm = value * inv_rms
            gather_taps(norm, put)
            step = times[0, micro]
            emb = table[pl.ds(step, 1), :]
            saved = jnp.where(hop, jnp.where(i == e, e, 2), i)
            for a, b in column_blocks(chans):
                pre = jnp.dot(lhs[...], w[slot, :, a:b], preferred_element_type=jnp.float32) + emb[:, a:b]
                sig = jax.nn.sigmoid(pre)
                branch = pre * sig
                result = value[:, a:b] + branch
                branch_b = branch.astype(jnp.bfloat16)
                result = result.astype(jnp.bfloat16).astype(jnp.float32)
                result = result + jnp.where(level == half - 1, branch_b.astype(jnp.float32), 0.0)
                fout[i, :, a:b] = result.astype(jnp.bfloat16)
                sout[i, :, a:b] = branch_b
                state[saved, :, chans + a : chans + b] = sig * (1.0 + pre * (1.0 - sig))

            @pl.when(sends_f(i))
            def _():
                copy_f(i).start()

            @pl.when(level < half - 1)
            def _():
                copy_s(i).start()

            @pl.when(jnp.logical_not(hop) & (i == 0))
            def _():
                inbox[1] = fout[0]

            state[saved, :, :chans] = norm
            state[saved, :, 2 * chans :] = jnp.broadcast_to(inv_rms, (PIX, 128))
            norm_b = norm.astype(jnp.bfloat16)

            @pl.when(hop | (i == e))
            def _():
                gathered[place, rows(micro * PIX, PIX), :] = norm_b

            @pl.when(jnp.logical_not(hop) & (i != e))
            def _():
                nstage[...] = norm_b
                copy_n(e).start()

            @pl.when(sends_t(i))
            def _():
                copy_t(e).start()

            return None

        lax.fori_loop(0, 2, forward, None)

        @pl.when(jnp.logical_not(top_line) & (line == line_len - 1))
        def _():
            for k in range(1, line_len):
                pl.semaphore_signal(go, inc=1, device_id=at(s - k, d))

        @pl.when(s < line_len)
        def _():
            turn_weights(e)

        @pl.when(jnp.logical_not(top_line) & (line < line_len - 1))
        def _():
            pl.semaphore_wait(go, 1)

        group = replicas // 2

        def copy_a(pz):
            ref = gathered.at[core * group + x * 2 + pz]
            return remote(ref, ref, a_send, a_recv, s, replica(x, 1 - zh, core))

        def copy_b(k, px):
            ref = gathered.at[pl.ds(core * group + px * 2, 2)]
            return remote(
                ref, ref, b_send.at[k - 1], b_recv.at[k - 1], s, replica(lax.rem(x + k, xs), zh, core))

        def copy_c(c):
            ref = gathered.at[pl.ds(c * group, group)]
            return remote(ref, ref, c_send, c_recv, s, sibling)

        tight = (s >= line_len) & jnp.logical_not(top_line)

        def gather_a():
            copy_a(zh).start()

        def gather_b():
            copy_a(1 - zh).wait_recv()
            for k in range(1, xs):
                copy_b(k, x).start()

        def gather_c():
            for k in range(1, xs):
                copy_b(k, lax.rem(x + xs - k, xs)).wait_recv()
            copy_c(core).start()
            copy_c(1 - core).wait_recv()

        def gather_all():
            copy_n(1 - e).wait_recv()
            gather_a()
            gather_b()
            gather_c()

        @pl.when(hop)
        def _():
            share_weights()
            gather_a()
            spread_z()

            @pl.when(jnp.logical_not(tight))
            def _():
                gather_b()

            spread_x()

            @pl.when(jnp.logical_not(tight))
            def _():
                gather_c()

            spread_y()

        @pl.when(jnp.logical_not(top_line))
        def _():
            turn_weights(1 - e)

        @pl.when(tight & jnp.logical_not(hop))
        def _():
            copy_n(1 - e).wait_recv()
            gather_a()

        @pl.when(hop)
        def _():
            copy_t(1 - e).wait_recv()

        low = lax.broadcasted_iota(jnp.int32, (1, lanes), 1) < PIX
        top_rows = ROWS // 2
        pad = jnp.zeros((ROWS - share, lanes), jnp.float32)
        pad_rows = jnp.zeros((PACK_ROWS - top_rows, lanes), jnp.float32)

        def pack_level(slot):
            for r in range(0, chans, 128):
                block = gpre[slot, :, r : r + 128]
                gtrans[r : r + 128, :] = jnp.concatenate([block, block], 0).T
            for j in range(replicas):
                first = gtrans[share * j : share * j + top_rows, :]
                rest = jnp.concatenate([gtrans[share * j + top_rows : share * (j + 1), :], pad], 0)
                block = jnp.concatenate([jnp.where(low, first, rest), pad_rows], 0)
                pack[slot, j] = block.astype(jnp.bfloat16)

        def copy_p(slot, to):
            index = slot * replicas + to
            return remote(
                pack.at[slot, to], shares.at[e, place], p_send.at[index], p_recv.at[e * replicas + place],
                2 * pair + slot, to)

        def share_dest(k):
            return replica(
                lax.rem(x + 1 + k // 2, xs), lax.rem(zh + 1 + k // (replicas // 2), 2), lax.rem(core + 1 + k, 2))

        def send_level(slot):
            pack_level(slot)

            def send_share(k, _):
                copy_p(slot, share_dest(k)).start()
                return None

            lax.fori_loop(0, jnp.where(slot == e, replicas - 1, replicas), send_share, None)

        def copy_g():
            return remote(gout.at[1], gin.at[0], g_send, g_recv, jnp.maximum(s - 2, 0), d)

        def copy_d(i):
            return remote(
                gout.at[i], dskip.at[i], d_send.at[i], d_recv.at[i], mirror(2 * pair + 1 - i, e), d)

        def wait_d(slot):
            remote(gout.at[0], dskip.at[slot], d_send.at[0], d_recv.at[slot], mate, d).wait_recv()

        def backward(i, _):
            slot = 1 - i
            level = 2 * pair + slot

            @pl.when((i == 0) & (pair < half - 1))
            def _():
                copy_g().wait_recv()

            @pl.when(level < half - 1)
            def _():
                wait_d(slot)

            grad = gin[i].astype(jnp.float32)
            factor = jnp.where(level == half - 1, 2.0, 1.0).astype(jnp.float32)
            branch_grad = grad * factor + dskip[slot].astype(jnp.float32)
            grad_pre = (branch_grad * state[slot, :, chans : 2 * chans]).astype(jnp.bfloat16).astype(jnp.float32)
            gpre[slot] = grad_pre

            @pl.when(level == 1)
            def _():
                send_level(1)

            @pl.when(level > 0)
            def _():
                gather_taps(grad_pre, put)
                parts = [
                    jnp.dot(lhs[...], wt[slot, :, a:b], preferred_element_type=jnp.float32)
                    for a, b in column_blocks(chans)
                ]
                gn = jnp.concatenate(parts, axis=1)
                norm = state[slot, :, :chans]
                inner = jnp.mean(gn * norm, axis=-1, keepdims=True)
                inv_rms = state[slot, :, 2 * chans : 2 * chans + 1]
                gout[i] = (grad + inv_rms * (gn - norm * inner)).astype(jnp.bfloat16)

            @pl.when((i == 1) & (pair > 0))
            def _():
                copy_g().start()

            @pl.when(level > half)
            def _():
                copy_d(i).start()

            @pl.when(i == 0)
            def _():
                gin[1] = gout[0]

            return None

        lax.fori_loop(0, 2, backward, None)

        @pl.when(pair > 0)
        def _():
            send_level(1)

        send_level(0)
        shares[e, place] = pack[e, d]

        @pl.when(tight)
        def _():
            gather_b()
            gather_c()

        @pl.when(top_line & (line < 2))
        def _():
            pl.semaphore_signal(go, inc=1, device_id=at(s + 2, d))

        @pl.when(top_line & (line >= 2))
        def _():
            pl.semaphore_wait(go, 1)

        @pl.when(top_line)
        def _():
            gather_all()

        copy_a(zh).wait_send()
        for k in range(1, xs):
            copy_b(k, x).wait_send()
        copy_c(core).wait_send()
        for k in range(6):
            copy_z(k).wait_send()
        for k in range(2):
            for n in range(1, xs):
                copy_v(n, k, x).wait_send()
            copy_y(k, core).wait_send()
        for k in range(4):
            copy_u(k, odd).wait_send()

        @pl.when(hop)
        def _():
            copy_t(e).wait_send()

        @pl.when(jnp.logical_not(hop))
        def _():
            copy_n(e).wait_send()

        @pl.when(pair > 0)
        def _():
            copy_g().wait_send()

        def drain(i, _):
            @pl.when(sends_f(i))
            def _():
                copy_f(i).wait_send()

            slot, micro = slot_and_micro(i)

            @pl.when(2 * pair + slot < half - 1)
            def _():
                copy_s(i).wait_send()

            @pl.when(2 * pair + 1 - i > half)
            def _():
                copy_d(i).wait_send()

            return None

        lax.fori_loop(0, 2, drain, None)

        def drain_share(k, _):
            to = lax.rem(d + k, replicas)
            copy_p(e, to).wait_send()
            copy_p(1 - e, to).wait_send()
            return None

        copy_p(1 - e, d).wait_send()
        lax.fori_loop(1, replicas, drain_share, None)

        def wait_share(micro, slot):
            remote(
                pack.at[0, 0], shares.at[micro, slot], p_send.at[0], p_recv.at[micro * replicas + slot], mate, d
            ).wait_recv()

        def wait_shares(k, _):
            slot = lax.rem(place + k, replicas)
            wait_share(0, slot)
            wait_share(1, slot)
            return None

        wait_share(1 - e, place)
        lax.fori_loop(1, replicas, wait_shares, None)

        lane = lax.broadcasted_iota(jnp.int32, (1, lanes), 1)
        row, col = (lane // SIDE) % SIDE, lane % SIDE
        keep = []
        for kh in range(3):
            for kw in range(3):
                r, c = row - (kh - 1), col - (kw - 1)
                keep.append((r >= 0) & (r < SIDE) & (c >= 0) & (c < SIDE))
        for b in range(replicas):
            one, two = (shares[m, b].astype(jnp.float32)[:top_rows] for m in range(2))
            block = jnp.concatenate(
                [jnp.where(low, one, pltpu.roll(two, PIX, 1)), jnp.where(low, pltpu.roll(one, PIX, 1), two)], 0)
            for t in range(9):
                shift = (SIDE * (t // 3 - 1) + t % 3 - 1) % lanes
                moved = pltpu.roll(block, shift, 1) if shift else block
                moved = jnp.where(keep[t], moved, 0.0)
                amat[ROWS * t : ROWS * (t + 1), lanes * b : lanes * (b + 1)] = moved.astype(jnp.bfloat16)
        rhs = gathered[...].reshape(replicas * lanes, chans)
        for a, b in column_blocks(chans):
            total = jnp.dot(amat[...], rhs[:, a:b], preferred_element_type=jnp.float32) * scale
            for t in range(9):
                out_ref[t, :, a:b] = total[ROWS * t : ROWS * t + share]


    return kernel


def on_device(latents, cotangent, conv_weight, timesteps, time_table):
    sections = lax.axis_size("section")
    replicas = lax.axis_size("dp")
    micro, samples, side_h, side_w, chans = latents.shape
    share = chans // replicas
    scale = 1.0 / math.sqrt(micro * samples * replicas * side_h * side_w)
    fields = (micro, PIX, chans)
    dma = pltpu.SemaphoreType.DMA
    anyspace = pl.BlockSpec(memory_space=pl.ANY)
    bf, f32 = jnp.bfloat16, jnp.float32
    out = pl.pallas_call(
        make_kernel(sections, replicas, chans, share, scale, PAIR_FROM),
        out_shape=jax.ShapeDtypeStruct((9, share, chans), f32),
        in_specs=[anyspace] * 5,
        out_specs=pl.BlockSpec(memory_space=pltpu.VMEM),
        scratch_shapes=[
            pltpu.SMEM((1, micro), jnp.int32),
            pltpu.VMEM((2, 9 * chans, chans), bf),
            pltpu.VMEM((2, 9 * chans, chans), bf),
            pltpu.VMEM(time_table.shape, f32),
            pltpu.VMEM((PIX, 9 * chans), bf),
            pltpu.VMEM(fields, bf),
            pltpu.VMEM(fields, bf),
            pltpu.VMEM(fields, bf),
            pltpu.VMEM(fields, bf),
            pltpu.VMEM(fields, bf),
            pltpu.VMEM(fields, bf),
            pltpu.VMEM(fields, bf),
            pltpu.VMEM((3, PIX, 2 * chans + 128), f32),
            pltpu.VMEM((2, PIX, chans), f32),
            pltpu.VMEM((chans, micro * PIX), f32),
            pltpu.VMEM((2, replicas, PACK_ROWS, micro * PIX), bf),
            pltpu.VMEM((2, replicas, PACK_ROWS, micro * PIX), bf),
            pltpu.VMEM((replicas, micro * PIX, chans), bf),
            pltpu.VMEM((PIX, chans), bf),
            pltpu.VMEM((9 * ROWS, replicas * micro * PIX), bf),
            dma((3,)), dma, dma((2,)), dma((2,)), dma((2,)), dma((2,)), dma, dma, dma((2,)), dma((2,)),
            dma, dma, dma((replicas // 4 - 1,)), dma((replicas // 4 - 1,)), dma, dma,
            dma((2 * replicas,)), dma((2 * replicas,)),
            dma, dma, dma, dma, dma((6,)), dma((6,)), dma((6,)), dma((6,)), dma((4,)), dma((4,)), dma((2,)), dma((2,)),
            pltpu.SemaphoreType.REGULAR,
        ],
        compiler_params=pltpu.CompilerParams(
            collective_id=0, has_side_effects=True, vmem_limit_bytes=56 * 2**20
        ),
        name="levels",
    )(
        timesteps.reshape(1, micro),
        latents.reshape(fields),
        cotangent.reshape(fields),
        conv_weight.reshape(9 * chans, chans),
        time_table,
    )
    return jnp.swapaxes(out, 1, 2).reshape(1, 3, 3, chans, share)


def solution(mesh):
    in_specs = (
        P(None, "dp", None, None, None),
        P(None, "dp", None, None, None),
        P("section", None, None, None, None),
        P(None, "dp"),
        P(),
    )
    out_specs = P("section", None, None, None, "dp")
    return jax.shard_map(
        on_device, mesh=mesh, in_specs=in_specs, out_specs=out_specs, check_vma=False
    )
```

```python
import math

import jax
import jax.numpy as jnp
from jax import lax
from jax.experimental import pallas as pl
from jax.experimental.pallas import tpu as pltpu
from jax.sharding import PartitionSpec as P

EPS = 1e-05
SIDE = 8
PIX = SIDE * SIDE
PAIR_FROM = 8
PACK_ROWS = 32
ROWS = 48


def gather_taps(value, store):
    chans = value.shape[1]
    col = lax.broadcasted_iota(jnp.int32, (PIX, 1), 0) % SIDE
    edge = jnp.zeros((SIDE, chans), jnp.float32)
    left = jnp.where(col > 0, pltpu.roll(value, 1, 0), 0.0)
    right = jnp.where(col < SIDE - 1, pltpu.roll(value, PIX - 1, 0), 0.0)
    for kw, v in enumerate((left, value, right)):
        store(kw, jnp.concatenate([edge, v[: PIX - SIDE]], 0).astype(jnp.bfloat16))
        store(3 + kw, v.astype(jnp.bfloat16))
        store(6 + kw, jnp.concatenate([v[SIDE:], edge], 0).astype(jnp.bfloat16))


def column_blocks(chans):
    return [(a, min(a + 256, chans)) for a in range(0, chans, 256)]


def make_kernel(sections, replicas, chans, share, scale, pair_from):
    half = sections // 2
    xs = replicas // 4
    lanes = 2 * PIX
    taps = 9 * chans

    def kernel(
        times_hbm, lat_ref, cot_ref, w_hbm, table_hbm, out_ref,
        times, w, wt, table, lhs, inbox, skip, fout, sout, gin, dskip, gout,
        state, gpre, gtrans, pack, shares, gathered, nstage, amat,
        load_sem, in_sem, f_send, f_recv, s_send, s_recv, g_send, g_recv, d_send, d_recv,
        a_send, a_recv, b_send, b_recv, c_send, c_recv, p_send, p_recv,
        n_send, n_recv, t_send, t_recv, z_send, z_recv, v_send, v_recv, u_send, u_recv, y_send, y_recv, go,
    ):
        s = lax.axis_index("section")
        d = lax.axis_index("dp")
        core = lax.rem(d, 2)
        zh = lax.rem(d // 2, 2)
        x = d // 4
        place = core * (replicas // 2) + x * 2 + zh
        pair, e = s // 2, lax.rem(s, 2)
        mate = s + 1 - 2 * e
        line_len = 4
        line = lax.rem(s, line_len)
        top_line = s >= sections - line_len
        hop = s < pair_from

        def at(dst_s, dst_d):
            return {"section": dst_s, "dp": dst_d}

        def replica(px, pz, pc):
            return px * 4 + pz * 2 + pc

        def remote(src, dst, send, recv, dst_s, dst_d):
            return pltpu.make_async_remote_copy(
                src_ref=src, dst_ref=dst, send_sem=send, recv_sem=recv, device_id=at(dst_s, dst_d))

        load_w = pltpu.make_async_copy(w_hbm, w.at[e], load_sem.at[0])
        load_t = pltpu.make_async_copy(table_hbm, table, load_sem.at[1])
        load_i = pltpu.make_async_copy(times_hbm, times, load_sem.at[2])
        load_w.start()
        load_t.start()
        load_i.start()

        barrier = pltpu.get_barrier_semaphore()

        def greet(k, _):
            to = lax.rem(d + k, replicas)
            pl.semaphore_signal(barrier, inc=1, device_id=at(s, to))
            pl.semaphore_signal(barrier, inc=1, device_id=at(mate, to))
            return None

        pl.semaphore_signal(barrier, inc=1, device_id=at(mate, d))
        lax.fori_loop(1, replicas, greet, None)
        relations = [
            (pair < half - 1, jnp.minimum(s + 2, sections - 1)),
            (pair > 0, jnp.maximum(s - 2, 0)),
            ((e == 1) & (s < pair_from), jnp.minimum(s + 1, sections - 1)),
            ((e == 0) & (s > 0) & (s <= pair_from), jnp.maximum(s - 1, 0)),
            (s >= 0, 2 * (half - 1 - pair) + e),
            ((s < pair_from) | (s >= sections - pair_from), sections - 1 - s),
            (line == line_len - 1, jnp.maximum(s - line_len + 1, 0)),
            (line == 0, jnp.minimum(s + line_len - 1, sections - 1)),
        ]
        expected = 2 * replicas - 1
        for wanted, other in relations:
            expected = expected + jnp.where(wanted, 1, 0)

            @pl.when(wanted)
            def _():
                pl.semaphore_signal(barrier, inc=1, device_id=at(other, d))

        @pl.when(s == 0)
        def _():
            load = pltpu.make_async_copy(lat_ref, inbox, in_sem)
            load.start()
            load.wait()

        @pl.when(pair == half - 1)
        def _():
            load = pltpu.make_async_copy(cot_ref.at[e], gin.at[0], in_sem)
            load.start()
            load.wait()

        @pl.when(s < half + 2)
        def _():
            skip[0] = jnp.zeros_like(skip[0])

        @pl.when(s < half)
        def _():
            skip[1] = jnp.zeros_like(skip[1])

        @pl.when(s >= half)
        def _():
            dskip[0] = jnp.zeros_like(dskip[0])

        @pl.when(s >= half - 2)
        def _():
            dskip[1] = jnp.zeros_like(dskip[1])

        pl.semaphore_wait(barrier, expected)

        def rows(start, count):
            return pl.ds(pl.multiple_of(start, 16), count)

        core_rows = taps // 2
        piece_v = core_rows // 16 // 16 * 16
        all_v = 8 * piece_v
        all_u = core_rows - all_v
        cut_u = [all_u // 2 * k // 4 // 16 * 16 for k in range(5)]
        size_u = [b - a for a, b in zip(cut_u, cut_u[1:])]
        base_v = core * core_rows + all_u
        odd = lax.rem(x, 2)
        sibling = replica(x, zh, 1 - core)

        def u_row(parity, k):
            return core * core_rows + parity * (all_u // 2) + cut_u[k]

        def v_row(px, k):
            return base_v + (2 * px + k) * piece_v

        def along(k):
            return replica(lax.rem(x + k, xs), zh, core)

        def copy_z(k):
            row, count = (v_row(x, k), piece_v) if k < 2 else (u_row(odd, k - 2), size_u[k - 2])
            return remote(
                w_hbm.at[rows(row, count)], w.at[e, rows(row, count)], z_send.at[k], z_recv.at[k], mate, d)

        def wait_z(k):
            row, count = (v_row(x, k), piece_v) if k < 2 else (u_row(odd, k - 2), size_u[k - 2])
            ref = w.at[1 - e, rows(row, count)]
            remote(ref, ref, z_send.at[k], z_recv.at[k], mate, d).wait_recv()

        def copy_v(n, k, px):
            ref = w.at[1 - e, rows(v_row(px, k), piece_v)]
            return remote(ref, ref, v_send.at[3 * k + n - 1], v_recv.at[3 * k + n - 1], s, along(n))

        def copy_u(k, parity):
            ref = w.at[1 - e, rows(u_row(parity, k), size_u[k])]
            return remote(ref, ref, u_send.at[k], u_recv.at[k], s, along(xs - 1 if k % 2 else 1))

        def copy_y(k, c):
            row, count = (c * core_rows + all_u, all_v) if k == 0 else (c * core_rows, all_u)
            ref = w.at[1 - e, rows(row, count)]
            return remote(ref, ref, y_send.at[k], y_recv.at[k], s, sibling)

        def share_weights():
            for k in range(6):
                copy_z(k).start()

        def spread_z():
            for k in range(2):
                wait_z(k)
                for n in (1, xs - 1, 2):
                    copy_v(n, k, x).start()

        def spread_x():
            for k in range(4):
                wait_z(2 + k)
                copy_u(k, odd).start()
            for k in range(2):
                for n in range(1, xs):
                    copy_v(n, k, lax.rem(x + xs - n, xs)).wait_recv()
            copy_y(0, core).start()
            for k in range(4):
                copy_u(k, 1 - odd).wait_recv()
            copy_y(1, core).start()

        def spread_y():
            for k in range(2):
                copy_y(k, 1 - core).wait_recv()

        def turn_weights(slot):
            def turn(t, _):
                src = pl.multiple_of(t * chans, chans)
                dst = pl.multiple_of((8 - t) * chans, chans)
                for r in range(0, chans, 128):
                    block = w[slot, pl.ds(src + r, 128), :]
                    wt[slot, pl.ds(dst, chans), r : r + 128] = block.T
                return None

            lax.fori_loop(0, 9, turn, None)

        @pl.when(s >= pair_from)
        def _():
            share_weights()

        load_w.wait()
        load_t.wait()
        load_i.wait()

        @pl.when(s >= line_len)
        def _():
            turn_weights(e)

        @pl.when(s >= pair_from)
        def _():
            spread_z()
            spread_x()
            spread_y()

        @pl.when(top_line)
        def _():
            turn_weights(1 - e)

        def put(t, v):
            lhs[:, t * chans : (t + 1) * chans] = v

        def slot_and_micro(i):
            return jnp.where(hop, e, i), jnp.where(hop, i, e)

        def mirror(level, micro):
            return 2 * ((sections - 1 - level) // 2) + micro

        def sends_f(i):
            return hop | ((i == 1) & (pair < half - 1))

        def copy_f(i):
            to = jnp.where(hop, jnp.where(s == pair_from - 1, pair_from + i, s + 1), jnp.minimum(s + 2, sections - 1))
            slot = jnp.where(s < pair_from - 1, i, 0)
            return remote(fout.at[i], inbox.at[slot], f_send.at[i], f_recv.at[slot], to, d)

        def wait_f(i):
            remote(fout.at[i], inbox.at[i], f_send.at[i], f_recv.at[i], mate, d).wait_recv()

        def copy_s(i):
            slot, micro = slot_and_micro(i)
            return remote(
                sout.at[i], skip.at[1 - slot], s_send.at[i], s_recv.at[1 - slot], mirror(2 * pair + slot, micro), d)

        def wait_s(slot):
            remote(sout.at[0], skip.at[slot], s_send.at[0], s_recv.at[slot], mate, d).wait_recv()

        def sends_t(i):
            return hop & (i != e)

        def copy_t(slot):
            return remote(state.at[2], state.at[slot], t_send, t_recv, mate, d)

        def copy_n(micro):
            return remote(
                nstage, gathered.at[place, rows(micro * PIX, PIX)], n_send, n_recv, mate, d)

        def forward(i, _):
            slot, micro = slot_and_micro(i)
            level = 2 * pair + slot

            @pl.when(jnp.where(hop, jnp.where(s > 0, 1, 0), 1 - i) == 1)
            def _():
                wait_f(i)

            @pl.when(level > half)
            def _():
                wait_s(slot)

            value = inbox[i].astype(jnp.float32) + skip[slot].astype(jnp.float32)
            inv_rms = lax.rsqrt(jnp.mean(value * value, axis=-1, keepdims=True) + EPS)
            norm = value * inv_rms
            gather_taps(norm, put)
            step = times[0, micro]
            emb = table[pl.ds(step, 1), :]
            saved = jnp.where(hop, jnp.where(i == e, e, 2), i)
            for a, b in column_blocks(chans):
                pre = jnp.dot(lhs[...], w[slot, :, a:b], preferred_element_type=jnp.float32) + emb[:, a:b]
                sig = jax.nn.sigmoid(pre)
                branch = pre * sig
                result = value[:, a:b] + branch
                branch_b = branch.astype(jnp.bfloat16)
                result = result.astype(jnp.bfloat16).astype(jnp.float32)
                result = result + jnp.where(level == half - 1, branch_b.astype(jnp.float32), 0.0)
                fout[i, :, a:b] = result.astype(jnp.bfloat16)
                sout[i, :, a:b] = branch_b
                state[saved, :, chans + a : chans + b] = sig * (1.0 + pre * (1.0 - sig))

            @pl.when(sends_f(i))
            def _():
                copy_f(i).start()

            @pl.when(jnp.logical_not(hop) & (i == 0))
            def _():
                inbox[1] = fout[0]

            state[saved, :, :chans] = norm
            state[saved, :, 2 * chans :] = jnp.broadcast_to(inv_rms, (PIX, 128))
            norm_b = norm.astype(jnp.bfloat16)

            @pl.when(hop | (i == e))
            def _():
                gathered[place, rows(micro * PIX, PIX), :] = norm_b

            @pl.when(jnp.logical_not(hop) & (i != e))
            def _():
                nstage[...] = norm_b

            return None

        lax.fori_loop(0, 2, forward, None)

        @pl.when(s < half - 1)
        def _():
            copy_s(0).start()
            copy_s(1).start()

        @pl.when(hop)
        def _():
            copy_t(e).start()

        @pl.when(jnp.logical_not(hop))
        def _():
            copy_n(e).start()

        @pl.when(jnp.logical_not(top_line) & (line == line_len - 1))
        def _():
            for k in range(1, line_len):
                pl.semaphore_signal(go, inc=1, device_id=at(s - k, d))

        @pl.when(s < line_len)
        def _():
            turn_weights(e)

        @pl.when(jnp.logical_not(top_line) & (line < line_len - 1))
        def _():
            pl.semaphore_wait(go, 1)

        group = replicas // 2

        def copy_a(pz):
            ref = gathered.at[core * group + x * 2 + pz]
            return remote(ref, ref, a_send, a_recv, s, replica(x, 1 - zh, core))

        def copy_b(k, px):
            ref = gathered.at[pl.ds(core * group + px * 2, 2)]
            return remote(
                ref, ref, b_send.at[k - 1], b_recv.at[k - 1], s, replica(lax.rem(x + k, xs), zh, core))

        def copy_c(c):
            ref = gathered.at[pl.ds(c * group, group)]
            return remote(ref, ref, c_send, c_recv, s, sibling)

        tight = (s >= line_len) & jnp.logical_not(top_line)

        def gather_a():
            copy_a(zh).start()

        def gather_b():
            copy_a(1 - zh).wait_recv()
            for k in range(1, xs):
                copy_b(k, x).start()

        def gather_c():
            for k in range(1, xs):
                copy_b(k, lax.rem(x + xs - k, xs)).wait_recv()
            copy_c(core).start()
            copy_c(1 - core).wait_recv()

        def gather_all():
            copy_n(1 - e).wait_recv()
            gather_a()
            gather_b()
            gather_c()

        @pl.when(hop)
        def _():
            share_weights()
            gather_a()
            spread_z()

            @pl.when(jnp.logical_not(tight))
            def _():
                gather_b()

            spread_x()

            @pl.when(jnp.logical_not(tight))
            def _():
                gather_c()

            spread_y()

        @pl.when(jnp.logical_not(top_line))
        def _():
            turn_weights(1 - e)

        @pl.when(tight & jnp.logical_not(hop))
        def _():
            copy_n(1 - e).wait_recv()
            gather_a()

        @pl.when(hop)
        def _():
            copy_t(1 - e).wait_recv()

        low = lax.broadcasted_iota(jnp.int32, (1, lanes), 1) < PIX
        top_rows = ROWS // 2
        pad = jnp.zeros((ROWS - share, lanes), jnp.float32)
        pad_rows = jnp.zeros((PACK_ROWS - top_rows, lanes), jnp.float32)

        def pack_level(slot):
            for r in range(0, chans, 128):
                block = gpre[slot, :, r : r + 128]
                gtrans[r : r + 128, :] = jnp.concatenate([block, block], 0).T
            for j in range(replicas):
                first = gtrans[share * j : share * j + top_rows, :]
                rest = jnp.concatenate([gtrans[share * j + top_rows : share * (j + 1), :], pad], 0)
                block = jnp.concatenate([jnp.where(low, first, rest), pad_rows], 0)
                pack[slot, j] = block.astype(jnp.bfloat16)

        def copy_p(slot, to):
            index = slot * replicas + to
            return remote(
                pack.at[slot, to], shares.at[e, place], p_send.at[index], p_recv.at[e * replicas + place],
                2 * pair + slot, to)

        def share_dest(k):
            return replica(
                lax.rem(x + 1 + k // 2, xs), lax.rem(zh + 1 + k // (replicas // 2), 2), lax.rem(core + 1 + k, 2))

        def send_level(slot):
            pack_level(slot)

            def send_share(k, _):
                copy_p(slot, share_dest(k)).start()
                return None

            lax.fori_loop(0, jnp.where(slot == e, replicas - 1, replicas), send_share, None)

        def copy_g():
            return remote(gout.at[1], gin.at[0], g_send, g_recv, jnp.maximum(s - 2, 0), d)

        def copy_d(i):
            return remote(
                gout.at[i], dskip.at[i], d_send.at[i], d_recv.at[i], mirror(2 * pair + 1 - i, e), d)

        def wait_d(slot):
            remote(gout.at[0], dskip.at[slot], d_send.at[0], d_recv.at[slot], mate, d).wait_recv()

        def backward(i, _):
            slot = 1 - i
            level = 2 * pair + slot

            @pl.when((i == 0) & (pair < half - 1))
            def _():
                copy_g().wait_recv()

            @pl.when(level < half - 1)
            def _():
                wait_d(slot)

            grad = gin[i].astype(jnp.float32)
            factor = jnp.where(level == half - 1, 2.0, 1.0).astype(jnp.float32)
            branch_grad = grad * factor + dskip[slot].astype(jnp.float32)
            grad_pre = (branch_grad * state[slot, :, chans : 2 * chans]).astype(jnp.bfloat16).astype(jnp.float32)
            gpre[slot] = grad_pre

            @pl.when(level == 1)
            def _():
                send_level(1)

            @pl.when(level > 0)
            def _():
                gather_taps(grad_pre, put)
                parts = [
                    jnp.dot(lhs[...], wt[slot, :, a:b], preferred_element_type=jnp.float32)
                    for a, b in column_blocks(chans)
                ]
                gn = jnp.concatenate(parts, axis=1)
                norm = state[slot, :, :chans]
                inner = jnp.mean(gn * norm, axis=-1, keepdims=True)
                inv_rms = state[slot, :, 2 * chans : 2 * chans + 1]
                gout[i] = (grad + inv_rms * (gn - norm * inner)).astype(jnp.bfloat16)

            @pl.when((i == 1) & (pair > 0))
            def _():
                copy_g().start()

            @pl.when(i == 0)
            def _():
                gin[1] = gout[0]

            return None

        lax.fori_loop(0, 2, backward, None)

        @pl.when(s >= half)
        def _():
            copy_d(0).start()

        @pl.when(s >= half + 2)
        def _():
            copy_d(1).start()

        @pl.when(pair > 0)
        def _():
            send_level(1)

        send_level(0)
        shares[e, place] = pack[e, d]

        @pl.when(tight)
        def _():
            gather_b()
            gather_c()

        @pl.when(top_line & (line < 2))
        def _():
            pl.semaphore_signal(go, inc=1, device_id=at(s + 2, d))

        @pl.when(top_line & (line >= 2))
        def _():
            pl.semaphore_wait(go, 1)

        @pl.when(top_line)
        def _():
            gather_all()

        copy_a(zh).wait_send()
        for k in range(1, xs):
            copy_b(k, x).wait_send()
        copy_c(core).wait_send()
        for k in range(6):
            copy_z(k).wait_send()
        for k in range(2):
            for n in range(1, xs):
                copy_v(n, k, x).wait_send()
            copy_y(k, core).wait_send()
        for k in range(4):
            copy_u(k, odd).wait_send()

        @pl.when(hop)
        def _():
            copy_t(e).wait_send()

        @pl.when(jnp.logical_not(hop))
        def _():
            copy_n(e).wait_send()

        @pl.when(pair > 0)
        def _():
            copy_g().wait_send()

        def drain(i, _):
            @pl.when(sends_f(i))
            def _():
                copy_f(i).wait_send()

            slot, micro = slot_and_micro(i)

            @pl.when(2 * pair + slot < half - 1)
            def _():
                copy_s(i).wait_send()

            @pl.when(2 * pair + 1 - i > half)
            def _():
                copy_d(i).wait_send()

            return None

        lax.fori_loop(0, 2, drain, None)

        def drain_share(k, _):
            to = lax.rem(d + k, replicas)
            copy_p(e, to).wait_send()
            copy_p(1 - e, to).wait_send()
            return None

        copy_p(1 - e, d).wait_send()
        lax.fori_loop(1, replicas, drain_share, None)

        def wait_share(micro, slot):
            remote(
                pack.at[0, 0], shares.at[micro, slot], p_send.at[0], p_recv.at[micro * replicas + slot], mate, d
            ).wait_recv()

        def wait_shares(k, _):
            slot = lax.rem(place + k, replicas)
            wait_share(0, slot)
            wait_share(1, slot)
            return None

        wait_share(1 - e, place)
        lax.fori_loop(1, replicas, wait_shares, None)

        lane = lax.broadcasted_iota(jnp.int32, (1, lanes), 1)
        row, col = (lane // SIDE) % SIDE, lane % SIDE
        keep = []
        for kh in range(3):
            for kw in range(3):
                r, c = row - (kh - 1), col - (kw - 1)
                keep.append((r >= 0) & (r < SIDE) & (c >= 0) & (c < SIDE))
        for b in range(replicas):
            one, two = (shares[m, b].astype(jnp.float32)[:top_rows] for m in range(2))
            block = jnp.concatenate(
                [jnp.where(low, one, pltpu.roll(two, PIX, 1)), jnp.where(low, pltpu.roll(one, PIX, 1), two)], 0)
            for t in range(9):
                shift = (SIDE * (t // 3 - 1) + t % 3 - 1) % lanes
                moved = pltpu.roll(block, shift, 1) if shift else block
                moved = jnp.where(keep[t], moved, 0.0)
                amat[ROWS * t : ROWS * (t + 1), lanes * b : lanes * (b + 1)] = moved.astype(jnp.bfloat16)
        rhs = gathered[...].reshape(replicas * lanes, chans)
        for a, b in column_blocks(chans):
            total = jnp.dot(amat[...], rhs[:, a:b], preferred_element_type=jnp.float32) * scale
            for t in range(9):
                out_ref[t, :, a:b] = total[ROWS * t : ROWS * t + share]


    return kernel


def on_device(latents, cotangent, conv_weight, timesteps, time_table):
    sections = lax.axis_size("section")
    replicas = lax.axis_size("dp")
    micro, samples, side_h, side_w, chans = latents.shape
    share = chans // replicas
    scale = 1.0 / math.sqrt(micro * samples * replicas * side_h * side_w)
    fields = (micro, PIX, chans)
    dma = pltpu.SemaphoreType.DMA
    anyspace = pl.BlockSpec(memory_space=pl.ANY)
    bf, f32 = jnp.bfloat16, jnp.float32
    out = pl.pallas_call(
        make_kernel(sections, replicas, chans, share, scale, PAIR_FROM),
        out_shape=jax.ShapeDtypeStruct((9, share, chans), f32),
        in_specs=[anyspace] * 5,
        out_specs=pl.BlockSpec(memory_space=pltpu.VMEM),
        scratch_shapes=[
            pltpu.SMEM((1, micro), jnp.int32),
            pltpu.VMEM((2, 9 * chans, chans), bf),
            pltpu.VMEM((2, 9 * chans, chans), bf),
            pltpu.VMEM(time_table.shape, f32),
            pltpu.VMEM((PIX, 9 * chans), bf),
            pltpu.VMEM(fields, bf),
            pltpu.VMEM(fields, bf),
            pltpu.VMEM(fields, bf),
            pltpu.VMEM(fields, bf),
            pltpu.VMEM(fields, bf),
            pltpu.VMEM(fields, bf),
            pltpu.VMEM(fields, bf),
            pltpu.VMEM((3, PIX, 2 * chans + 128), f32),
            pltpu.VMEM((2, PIX, chans), f32),
            pltpu.VMEM((chans, micro * PIX), f32),
            pltpu.VMEM((2, replicas, PACK_ROWS, micro * PIX), bf),
            pltpu.VMEM((2, replicas, PACK_ROWS, micro * PIX), bf),
            pltpu.VMEM((replicas, micro * PIX, chans), bf),
            pltpu.VMEM((PIX, chans), bf),
            pltpu.VMEM((9 * ROWS, replicas * micro * PIX), bf),
            dma((3,)), dma, dma((2,)), dma((2,)), dma((2,)), dma((2,)), dma, dma, dma((2,)), dma((2,)),
            dma, dma, dma((replicas // 4 - 1,)), dma((replicas // 4 - 1,)), dma, dma,
            dma((2 * replicas,)), dma((2 * replicas,)),
            dma, dma, dma, dma, dma((6,)), dma((6,)), dma((6,)), dma((6,)), dma((4,)), dma((4,)), dma((2,)), dma((2,)),
            pltpu.SemaphoreType.REGULAR,
        ],
        compiler_params=pltpu.CompilerParams(
            collective_id=0, has_side_effects=True, vmem_limit_bytes=56 * 2**20
        ),
        name="levels",
    )(
        timesteps.reshape(1, micro),
        latents.reshape(fields),
        cotangent.reshape(fields),
        conv_weight.reshape(9 * chans, chans),
        time_table,
    )
    return jnp.swapaxes(out, 1, 2).reshape(1, 3, 3, chans, share)


def solution(mesh):
    in_specs = (
        P(None, "dp", None, None, None),
        P(None, "dp", None, None, None),
        P("section", None, None, None, None),
        P(None, "dp"),
        P(),
    )
    out_specs = P("section", None, None, None, "dp")
    return jax.shard_map(
        on_device, mesh=mesh, in_specs=in_specs, out_specs=out_specs, check_vma=False
    )
```

```python
import math

import jax
import jax.numpy as jnp
from jax import lax
from jax.experimental import pallas as pl
from jax.experimental.pallas import tpu as pltpu
from jax.sharding import PartitionSpec as P

EPS = 1e-05
SIDE = 8
PIX = SIDE * SIDE
PAIR_FROM = 8
PACK_ROWS = 32
ROWS = 48


def gather_taps(value, store):
    chans = value.shape[1]
    col = lax.broadcasted_iota(jnp.int32, (PIX, 1), 0) % SIDE
    edge = jnp.zeros((SIDE, chans), jnp.float32)
    left = jnp.where(col > 0, pltpu.roll(value, 1, 0), 0.0)
    right = jnp.where(col < SIDE - 1, pltpu.roll(value, PIX - 1, 0), 0.0)
    for kw, v in enumerate((left, value, right)):
        store(kw, jnp.concatenate([edge, v[: PIX - SIDE]], 0).astype(jnp.bfloat16))
        store(3 + kw, v.astype(jnp.bfloat16))
        store(6 + kw, jnp.concatenate([v[SIDE:], edge], 0).astype(jnp.bfloat16))


def column_blocks(chans):
    return [(a, min(a + 256, chans)) for a in range(0, chans, 256)]


def make_kernel(sections, replicas, chans, share, scale, pair_from):
    half = sections // 2
    xs = replicas // 4
    lanes = 2 * PIX
    taps = 9 * chans

    def kernel(
        times_hbm, lat_ref, cot_ref, w_hbm, table_hbm, out_ref,
        times, w, wt, table, lhs, inbox, skip, fout, sout, gin, dskip, gout,
        state, gpre, gtrans, pack, shares, gathered, nstage, amat,
        load_sem, in_sem, f_send, f_recv, s_send, s_recv, g_send, g_recv, d_send, d_recv,
        a_send, a_recv, b_send, b_recv, c_send, c_recv, p_send, p_recv,
        n_send, n_recv, t_send, t_recv, z_send, z_recv, v_send, v_recv, u_send, u_recv, y_send, y_recv, go,
    ):
        s = lax.axis_index("section")
        d = lax.axis_index("dp")
        core = lax.rem(d, 2)
        zh = lax.rem(d // 2, 2)
        x = d // 4
        place = core * (replicas // 2) + x * 2 + zh
        pair, e = s // 2, lax.rem(s, 2)
        mate = s + 1 - 2 * e
        line_len = 4
        line = lax.rem(s, line_len)
        top_line = s >= sections - line_len
        hop = s < pair_from

        def at(dst_s, dst_d):
            return {"section": dst_s, "dp": dst_d}

        def replica(px, pz, pc):
            return px * 4 + pz * 2 + pc

        def remote(src, dst, send, recv, dst_s, dst_d):
            return pltpu.make_async_remote_copy(
                src_ref=src, dst_ref=dst, send_sem=send, recv_sem=recv, device_id=at(dst_s, dst_d))

        load_w = pltpu.make_async_copy(w_hbm, w.at[e], load_sem.at[0])
        load_t = pltpu.make_async_copy(table_hbm, table, load_sem.at[1])
        load_i = pltpu.make_async_copy(times_hbm, times, load_sem.at[2])
        load_w.start()
        load_t.start()
        load_i.start()

        barrier = pltpu.get_barrier_semaphore()

        def greet(k, _):
            to = lax.rem(d + k, replicas)
            pl.semaphore_signal(barrier, inc=1, device_id=at(s, to))
            pl.semaphore_signal(barrier, inc=1, device_id=at(mate, to))
            return None

        pl.semaphore_signal(barrier, inc=1, device_id=at(mate, d))
        lax.fori_loop(1, replicas, greet, None)
        relations = [
            (pair < half - 1, jnp.minimum(s + 2, sections - 1)),
            (pair > 0, jnp.maximum(s - 2, 0)),
            ((e == 1) & (s < pair_from), jnp.minimum(s + 1, sections - 1)),
            ((e == 0) & (s > 0) & (s <= pair_from), jnp.maximum(s - 1, 0)),
            (s >= 0, 2 * (half - 1 - pair) + e),
            ((s < pair_from) | (s >= sections - pair_from), sections - 1 - s),
            (line == line_len - 1, jnp.maximum(s - line_len + 1, 0)),
            (line == 0, jnp.minimum(s + line_len - 1, sections - 1)),
        ]
        expected = 2 * replicas - 1
        for wanted, other in relations:
            expected = expected + jnp.where(wanted, 1, 0)

            @pl.when(wanted)
            def _():
                pl.semaphore_signal(barrier, inc=1, device_id=at(other, d))

        @pl.when(s == 0)
        def _():
            load = pltpu.make_async_copy(lat_ref, inbox, in_sem)
            load.start()
            load.wait()

        @pl.when(pair == half - 1)
        def _():
            load = pltpu.make_async_copy(cot_ref.at[e], gin.at[0], in_sem)
            load.start()
            load.wait()

        @pl.when(s < half + 2)
        def _():
            skip[0] = jnp.zeros_like(skip[0])

        @pl.when(s < half)
        def _():
            skip[1] = jnp.zeros_like(skip[1])

        @pl.when(s >= half)
        def _():
            dskip[0] = jnp.zeros_like(dskip[0])

        @pl.when(s >= half - 2)
        def _():
            dskip[1] = jnp.zeros_like(dskip[1])

        pl.semaphore_wait(barrier, expected)

        def rows(start, count):
            return pl.ds(pl.multiple_of(start, 16), count)

        core_rows = taps // 2
        piece_v = core_rows // 16 // 16 * 16
        all_v = 8 * piece_v
        all_u = core_rows - all_v
        cut_u = [all_u // 2 * k // 4 // 16 * 16 for k in range(5)]
        size_u = [b - a for a, b in zip(cut_u, cut_u[1:])]
        base_v = core * core_rows + all_u
        odd = lax.rem(x, 2)
        sibling = replica(x, zh, 1 - core)

        def u_row(parity, k):
            return core * core_rows + parity * (all_u // 2) + cut_u[k]

        def v_row(px, k):
            return base_v + (2 * px + k) * piece_v

        def along(k):
            return replica(lax.rem(x + k, xs), zh, core)

        def copy_z(k):
            row, count = (v_row(x, k), piece_v) if k < 2 else (u_row(odd, k - 2), size_u[k - 2])
            return remote(
                w_hbm.at[rows(row, count)], w.at[e, rows(row, count)], z_send.at[k], z_recv.at[k], mate, d)

        def wait_z(k):
            row, count = (v_row(x, k), piece_v) if k < 2 else (u_row(odd, k - 2), size_u[k - 2])
            ref = w.at[1 - e, rows(row, count)]
            remote(ref, ref, z_send.at[k], z_recv.at[k], mate, d).wait_recv()

        def copy_v(n, k, px):
            ref = w.at[1 - e, rows(v_row(px, k), piece_v)]
            return remote(ref, ref, v_send.at[3 * k + n - 1], v_recv.at[3 * k + n - 1], s, along(n))

        def copy_u(k, parity):
            ref = w.at[1 - e, rows(u_row(parity, k), size_u[k])]
            return remote(ref, ref, u_send.at[k], u_recv.at[k], s, along(xs - 1 if k % 2 else 1))

        def copy_y(k, c):
            row, count = (c * core_rows + all_u, all_v) if k == 0 else (c * core_rows, all_u)
            ref = w.at[1 - e, rows(row, count)]
            return remote(ref, ref, y_send.at[k], y_recv.at[k], s, sibling)

        def share_weights():
            for k in range(6):
                copy_z(k).start()

        def spread_z():
            for k in range(2):
                wait_z(k)
                for n in (2, 1, xs - 1):
                    copy_v(n, k, x).start()

        def spread_x():
            for k in range(4):
                wait_z(2 + k)
                copy_u(k, odd).start()
            for k in range(2):
                for n in range(1, xs):
                    copy_v(n, k, lax.rem(x + xs - n, xs)).wait_recv()
            copy_y(0, core).start()
            for k in range(4):
                copy_u(k, 1 - odd).wait_recv()
            copy_y(1, core).start()

        def spread_y():
            for k in range(2):
                copy_y(k, 1 - core).wait_recv()

        def turn_weights(slot):
            def turn(t, _):
                src = pl.multiple_of(t * chans, chans)
                dst = pl.multiple_of((8 - t) * chans, chans)
                for r in range(0, chans, 128):
                    block = w[slot, pl.ds(src + r, 128), :]
                    wt[slot, pl.ds(dst, chans), r : r + 128] = block.T
                return None

            lax.fori_loop(0, 9, turn, None)

        @pl.when(s >= pair_from)
        def _():
            share_weights()

        load_w.wait()
        load_t.wait()
        load_i.wait()

        @pl.when(s >= pair_from)
        def _():
            spread_z()

        @pl.when(s >= line_len)
        def _():
            turn_weights(e)

        @pl.when(s >= pair_from)
        def _():
            spread_x()
            spread_y()

        @pl.when(top_line)
        def _():
            turn_weights(1 - e)

        def put(t, v):
            lhs[:, t * chans : (t + 1) * chans] = v

        def slot_and_micro(i):
            return jnp.where(hop, e, i), jnp.where(hop, i, e)

        def mirror(level, micro):
            return 2 * ((sections - 1 - level) // 2) + micro

        def sends_f(i):
            return hop | ((i == 1) & (pair < half - 1))

        def copy_f(i):
            to = jnp.where(hop, jnp.where(s == pair_from - 1, pair_from + i, s + 1), jnp.minimum(s + 2, sections - 1))
            slot = jnp.where(s < pair_from - 1, i, 0)
            return remote(fout.at[i], inbox.at[slot], f_send.at[i], f_recv.at[slot], to, d)

        def wait_f(i):
            remote(fout.at[i], inbox.at[i], f_send.at[i], f_recv.at[i], mate, d).wait_recv()

        def copy_s(i):
            slot, micro = slot_and_micro(i)
            return remote(
                sout.at[i], skip.at[1 - slot], s_send.at[i], s_recv.at[1 - slot], mirror(2 * pair + slot, micro), d)

        def wait_s(slot):
            remote(sout.at[0], skip.at[slot], s_send.at[0], s_recv.at[slot], mate, d).wait_recv()

        def sends_t(i):
            return hop & (i != e)

        def copy_t(slot):
            return remote(state.at[2], state.at[slot], t_send, t_recv, mate, d)

        def copy_n(micro):
            return remote(
                nstage, gathered.at[place, rows(micro * PIX, PIX)], n_send, n_recv, mate, d)

        def forward(i, _):
            slot, micro = slot_and_micro(i)
            level = 2 * pair + slot

            @pl.when(jnp.where(hop, jnp.where(s > 0, 1, 0), 1 - i) == 1)
            def _():
                wait_f(i)

            @pl.when(level > half)
            def _():
                wait_s(slot)

            value = inbox[i].astype(jnp.float32) + skip[slot].astype(jnp.float32)
            inv_rms = lax.rsqrt(jnp.mean(value * value, axis=-1, keepdims=True) + EPS)
            norm = value * inv_rms
            gather_taps(norm, put)
            step = times[0, micro]
            emb = table[pl.ds(step, 1), :]
            saved = jnp.where(hop, jnp.where(i == e, e, 2), i)
            for a, b in column_blocks(chans):
                pre = jnp.dot(lhs[...], w[slot, :, a:b], preferred_element_type=jnp.float32) + emb[:, a:b]
                sig = jax.nn.sigmoid(pre)
                branch = pre * sig
                result = value[:, a:b] + branch
                branch_b = branch.astype(jnp.bfloat16)
                result = result.astype(jnp.bfloat16).astype(jnp.float32)
                result = result + jnp.where(level == half - 1, branch_b.astype(jnp.float32), 0.0)
                fout[i, :, a:b] = result.astype(jnp.bfloat16)
                sout[i, :, a:b] = branch_b
                state[saved, :, chans + a : chans + b] = sig * (1.0 + pre * (1.0 - sig))

            @pl.when(sends_f(i))
            def _():
                copy_f(i).start()

            @pl.when(jnp.logical_not(hop) & (i == 0))
            def _():
                inbox[1] = fout[0]

            state[saved, :, :chans] = norm
            state[saved, :, 2 * chans :] = jnp.broadcast_to(inv_rms, (PIX, 128))
            norm_b = norm.astype(jnp.bfloat16)

            @pl.when(hop | (i == e))
            def _():
                gathered[place, rows(micro * PIX, PIX), :] = norm_b

            @pl.when(jnp.logical_not(hop) & (i != e))
            def _():
                nstage[...] = norm_b

            return None

        lax.fori_loop(0, 2, forward, None)

        @pl.when(s < half - 1)
        def _():
            copy_s(0).start()
            copy_s(1).start()

        @pl.when(hop)
        def _():
            copy_t(e).start()

        @pl.when(jnp.logical_not(hop))
        def _():
            copy_n(e).start()

        @pl.when(jnp.logical_not(top_line) & (line == line_len - 1))
        def _():
            for k in range(1, line_len):
                pl.semaphore_signal(go, inc=1, device_id=at(s - k, d))

        @pl.when(s < line_len)
        def _():
            turn_weights(e)

        @pl.when(jnp.logical_not(top_line) & (line < line_len - 1))
        def _():
            pl.semaphore_wait(go, 1)

        group = replicas // 2

        def copy_a(pz):
            ref = gathered.at[core * group + x * 2 + pz]
            return remote(ref, ref, a_send, a_recv, s, replica(x, 1 - zh, core))

        def copy_b(k, px):
            ref = gathered.at[pl.ds(core * group + px * 2, 2)]
            return remote(
                ref, ref, b_send.at[k - 1], b_recv.at[k - 1], s, replica(lax.rem(x + k, xs), zh, core))

        def copy_c(c):
            ref = gathered.at[pl.ds(c * group, group)]
            return remote(ref, ref, c_send, c_recv, s, sibling)

        tight = (s >= line_len) & jnp.logical_not(top_line)

        def gather_a():
            copy_a(zh).start()

        def gather_b():
            copy_a(1 - zh).wait_recv()
            for k in range(1, xs):
                copy_b(k, x).start()

        def gather_c():
            for k in range(1, xs):
                copy_b(k, lax.rem(x + xs - k, xs)).wait_recv()
            copy_c(core).start()
            copy_c(1 - core).wait_recv()

        def gather_all():
            copy_n(1 - e).wait_recv()
            gather_a()
            gather_b()
            gather_c()

        @pl.when(hop)
        def _():
            share_weights()
            gather_a()
            spread_z()

            @pl.when(jnp.logical_not(tight))
            def _():
                gather_b()

            spread_x()

            @pl.when(jnp.logical_not(tight))
            def _():
                gather_c()

            spread_y()

        @pl.when(jnp.logical_not(top_line))
        def _():
            turn_weights(1 - e)

        @pl.when(tight & jnp.logical_not(hop))
        def _():
            copy_n(1 - e).wait_recv()
            gather_a()

        @pl.when(hop)
        def _():
            copy_t(1 - e).wait_recv()

        low = lax.broadcasted_iota(jnp.int32, (1, lanes), 1) < PIX
        top_rows = ROWS // 2
        pad = jnp.zeros((ROWS - share, lanes), jnp.float32)
        pad_rows = jnp.zeros((PACK_ROWS - top_rows, lanes), jnp.float32)

        def pack_level(slot):
            for r in range(0, chans, 128):
                block = gpre[slot, :, r : r + 128]
                gtrans[r : r + 128, :] = jnp.concatenate([block, block], 0).T
            for j in range(replicas):
                first = gtrans[share * j : share * j + top_rows, :]
                rest = jnp.concatenate([gtrans[share * j + top_rows : share * (j + 1), :], pad], 0)
                block = jnp.concatenate([jnp.where(low, first, rest), pad_rows], 0)
                pack[slot, j] = block.astype(jnp.bfloat16)

        def copy_p(slot, to):
            index = slot * replicas + to
            return remote(
                pack.at[slot, to], shares.at[e, place], p_send.at[index], p_recv.at[e * replicas + place],
                2 * pair + slot, to)

        def share_dest(k):
            return replica(
                lax.rem(x + 1 + k // 2, xs), lax.rem(zh + 1 + k // (replicas // 2), 2), lax.rem(core + 1 + k, 2))

        def send_level(slot):
            pack_level(slot)

            def send_share(k, _):
                copy_p(slot, share_dest(k)).start()
                return None

            lax.fori_loop(0, jnp.where(slot == e, replicas - 1, replicas), send_share, None)

        def copy_g():
            return remote(gout.at[1], gin.at[0], g_send, g_recv, jnp.maximum(s - 2, 0), d)

        def copy_d(i):
            return remote(
                gout.at[i], dskip.at[i], d_send.at[i], d_recv.at[i], mirror(2 * pair + 1 - i, e), d)

        def wait_d(slot):
            remote(gout.at[0], dskip.at[slot], d_send.at[0], d_recv.at[slot], mate, d).wait_recv()

        def backward(i, _):
            slot = 1 - i
            level = 2 * pair + slot

            @pl.when((i == 0) & (pair < half - 1))
            def _():
                copy_g().wait_recv()

            @pl.when(level < half - 1)
            def _():
                wait_d(slot)

            grad = gin[i].astype(jnp.float32)
            factor = jnp.where(level == half - 1, 2.0, 1.0).astype(jnp.float32)
            branch_grad = grad * factor + dskip[slot].astype(jnp.float32)
            grad_pre = (branch_grad * state[slot, :, chans : 2 * chans]).astype(jnp.bfloat16).astype(jnp.float32)
            gpre[slot] = grad_pre

            @pl.when(level == 1)
            def _():
                send_level(1)

            @pl.when(level > 0)
            def _():
                gather_taps(grad_pre, put)
                parts = [
                    jnp.dot(lhs[...], wt[slot, :, a:b], preferred_element_type=jnp.float32)
                    for a, b in column_blocks(chans)
                ]
                gn = jnp.concatenate(parts, axis=1)
                norm = state[slot, :, :chans]
                inner = jnp.mean(gn * norm, axis=-1, keepdims=True)
                inv_rms = state[slot, :, 2 * chans : 2 * chans + 1]
                gout[i] = (grad + inv_rms * (gn - norm * inner)).astype(jnp.bfloat16)

            @pl.when((i == 1) & (pair > 0))
            def _():
                copy_g().start()

            @pl.when(i == 0)
            def _():
                gin[1] = gout[0]

            return None

        lax.fori_loop(0, 2, backward, None)

        @pl.when(s >= half)
        def _():
            copy_d(0).start()

        @pl.when(s >= half + 2)
        def _():
            copy_d(1).start()

        @pl.when(pair > 0)
        def _():
            send_level(1)

        send_level(0)
        shares[e, place] = pack[e, d]

        @pl.when(tight)
        def _():
            gather_b()
            gather_c()

        @pl.when(top_line & (line < 2))
        def _():
            pl.semaphore_signal(go, inc=1, device_id=at(s + 2, d))

        @pl.when(top_line & (line >= 2))
        def _():
            pl.semaphore_wait(go, 1)

        @pl.when(top_line)
        def _():
            gather_all()

        copy_a(zh).wait_send()
        for k in range(1, xs):
            copy_b(k, x).wait_send()
        copy_c(core).wait_send()
        for k in range(6):
            copy_z(k).wait_send()
        for k in range(2):
            for n in range(1, xs):
                copy_v(n, k, x).wait_send()
            copy_y(k, core).wait_send()
        for k in range(4):
            copy_u(k, odd).wait_send()

        @pl.when(hop)
        def _():
            copy_t(e).wait_send()

        @pl.when(jnp.logical_not(hop))
        def _():
            copy_n(e).wait_send()

        @pl.when(pair > 0)
        def _():
            copy_g().wait_send()

        def drain(i, _):
            @pl.when(sends_f(i))
            def _():
                copy_f(i).wait_send()

            slot, micro = slot_and_micro(i)

            @pl.when(2 * pair + slot < half - 1)
            def _():
                copy_s(i).wait_send()

            @pl.when(2 * pair + 1 - i > half)
            def _():
                copy_d(i).wait_send()

            return None

        lax.fori_loop(0, 2, drain, None)

        def drain_share(k, _):
            to = lax.rem(d + k, replicas)
            copy_p(e, to).wait_send()
            copy_p(1 - e, to).wait_send()
            return None

        copy_p(1 - e, d).wait_send()
        lax.fori_loop(1, replicas, drain_share, None)

        def wait_share(micro, slot):
            remote(
                pack.at[0, 0], shares.at[micro, slot], p_send.at[0], p_recv.at[micro * replicas + slot], mate, d
            ).wait_recv()

        def wait_shares(k, _):
            slot = lax.rem(place + k, replicas)
            wait_share(0, slot)
            wait_share(1, slot)
            return None

        wait_share(1 - e, place)
        lax.fori_loop(1, replicas, wait_shares, None)

        lane = lax.broadcasted_iota(jnp.int32, (1, lanes), 1)
        row, col = (lane // SIDE) % SIDE, lane % SIDE
        keep = []
        for kh in range(3):
            for kw in range(3):
                r, c = row - (kh - 1), col - (kw - 1)
                keep.append((r >= 0) & (r < SIDE) & (c >= 0) & (c < SIDE))
        for b in range(replicas):
            one, two = (shares[m, b].astype(jnp.float32)[:top_rows] for m in range(2))
            block = jnp.concatenate(
                [jnp.where(low, one, pltpu.roll(two, PIX, 1)), jnp.where(low, pltpu.roll(one, PIX, 1), two)], 0)
            for t in range(9):
                shift = (SIDE * (t // 3 - 1) + t % 3 - 1) % lanes
                moved = pltpu.roll(block, shift, 1) if shift else block
                moved = jnp.where(keep[t], moved, 0.0)
                amat[ROWS * t : ROWS * (t + 1), lanes * b : lanes * (b + 1)] = moved.astype(jnp.bfloat16)
        rhs = gathered[...].reshape(replicas * lanes, chans)
        for a, b in column_blocks(chans):
            total = jnp.dot(amat[...], rhs[:, a:b], preferred_element_type=jnp.float32) * scale
            for t in range(9):
                out_ref[t, :, a:b] = total[ROWS * t : ROWS * t + share]


    return kernel


def on_device(latents, cotangent, conv_weight, timesteps, time_table):
    sections = lax.axis_size("section")
    replicas = lax.axis_size("dp")
    micro, samples, side_h, side_w, chans = latents.shape
    share = chans // replicas
    scale = 1.0 / math.sqrt(micro * samples * replicas * side_h * side_w)
    fields = (micro, PIX, chans)
    dma = pltpu.SemaphoreType.DMA
    anyspace = pl.BlockSpec(memory_space=pl.ANY)
    bf, f32 = jnp.bfloat16, jnp.float32
    out = pl.pallas_call(
        make_kernel(sections, replicas, chans, share, scale, PAIR_FROM),
        out_shape=jax.ShapeDtypeStruct((9, share, chans), f32),
        in_specs=[anyspace] * 5,
        out_specs=pl.BlockSpec(memory_space=pltpu.VMEM),
        scratch_shapes=[
            pltpu.SMEM((1, micro), jnp.int32),
            pltpu.VMEM((2, 9 * chans, chans), bf),
            pltpu.VMEM((2, 9 * chans, chans), bf),
            pltpu.VMEM(time_table.shape, f32),
            pltpu.VMEM((PIX, 9 * chans), bf),
            pltpu.VMEM(fields, bf),
            pltpu.VMEM(fields, bf),
            pltpu.VMEM(fields, bf),
            pltpu.VMEM(fields, bf),
            pltpu.VMEM(fields, bf),
            pltpu.VMEM(fields, bf),
            pltpu.VMEM(fields, bf),
            pltpu.VMEM((3, PIX, 2 * chans + 128), f32),
            pltpu.VMEM((2, PIX, chans), f32),
            pltpu.VMEM((chans, micro * PIX), f32),
            pltpu.VMEM((2, replicas, PACK_ROWS, micro * PIX), bf),
            pltpu.VMEM((2, replicas, PACK_ROWS, micro * PIX), bf),
            pltpu.VMEM((replicas, micro * PIX, chans), bf),
            pltpu.VMEM((PIX, chans), bf),
            pltpu.VMEM((9 * ROWS, replicas * micro * PIX), bf),
            dma((3,)), dma, dma((2,)), dma((2,)), dma((2,)), dma((2,)), dma, dma, dma((2,)), dma((2,)),
            dma, dma, dma((replicas // 4 - 1,)), dma((replicas // 4 - 1,)), dma, dma,
            dma((2 * replicas,)), dma((2 * replicas,)),
            dma, dma, dma, dma, dma((6,)), dma((6,)), dma((6,)), dma((6,)), dma((4,)), dma((4,)), dma((2,)), dma((2,)),
            pltpu.SemaphoreType.REGULAR,
        ],
        compiler_params=pltpu.CompilerParams(
            collective_id=0, has_side_effects=True, vmem_limit_bytes=56 * 2**20
        ),
        name="levels",
    )(
        timesteps.reshape(1, micro),
        latents.reshape(fields),
        cotangent.reshape(fields),
        conv_weight.reshape(9 * chans, chans),
        time_table,
    )
    return jnp.swapaxes(out, 1, 2).reshape(1, 3, 3, chans, share)


def solution(mesh):
    in_specs = (
        P(None, "dp", None, None, None),
        P(None, "dp", None, None, None),
        P("section", None, None, None, None),
        P(None, "dp"),
        P(),
    )
    out_specs = P("section", None, None, None, "dp")
    return jax.shard_map(
        on_device, mesh=mesh, in_specs=in_specs, out_specs=out_specs, check_vma=False
    )
```
